32 devices in a mesh: groups: 2 (over y), wide: 4 (over x, core), rows: 4 (over z).
Axes of the slice: x: 2, y: 2, z: 4, core: 2. Of those that a mesh axis runs over, the one named last changes fastest.
Arguments:
- features: bfloat16 [256, 24576], P('wide', ('groups', 'rows')), parts along dimension 1, may hold values from -6 to 6
- tile_weights: bfloat16 [1920, 128, 128], P(('groups', 'rows')), parts along dimension 0, may hold values from -0.25 to 0.25
- tile_source: int32 [1920], P(('groups', 'rows')), parts along dimension 0, may hold values from 0 to 23
- tile_dest: int32 [1920], P(('groups', 'rows')), parts along dimension 0, may hold values from 0 to 95, as said below
- tile_count: int32 [8], P(('groups', 'rows')), parts along dimension 0, may hold values from 1 to 240, as said below
- weight: bfloat16 [256, 256], replicated, may hold values from -0.375 to 0.375
- bias: bfloat16 [256], replicated, may hold values from -3 to 3
- cotangent: bfloat16 [24576, 256], P(('groups', 'rows', 'wide')), parts along dimension 0, may hold values from -6 to 6
Outputs:
- activation: bfloat16 [24576, 256], P(('groups', 'rows', 'wide')), parts along dimension 0
- grad_features: bfloat16 [256, 24576], P('wide', ('groups', 'rows')), parts along dimension 1
- grad_weight: float32 [512, 256], P('groups'), parts along dimension 0
- grad_bias: float32 [512], P('groups'), parts along dimension 0
The draws below stay inside these ranges and needn't reach their ends.
There are 2 independent parts, one for each index of `groups`. The reference program is written for one: setup_inputs(seed, part) draws one part's arguments, and reference() takes and returns one part's arrays. A program takes and returns all parts, laid end to end along the dimension named above; an argument that names none is the same for every part. Nothing has to cross between parts.
Inputs may be any that keep to these rules, and one draw needn't show every extreme that they name: `tile_dest`: destination row block of each tile; a block may receive tiles from slots of several indices of rows. `tile_count`: live tile slots of one index of rows; in every draw some index has all 240 slots live.
All inputs are finite; a program needn't handle non-finite values.
Results may differ from the reference program's by a relative error of at most 0.0062.
Values may be sent and summed in bfloat16 or wider, within the bound.
No kernel may reach another device: no remote copies, remote signals or barrier semaphores. Data moves between devices by JAX's collectives and lax.ppermute only.
A program may use at most 128 MiB of HBM per device.

```python
import jax
import jax.numpy as jnp
from jax import lax

F = 256
BLK = 128
TPB = 10
SB_DEV = 24
BLOCKS = 96
NODES = 12288
TILE_DEV = 240
NT = 960
N_ROWS = 4


def draw_tile_dest(key, part):
    key = jax.random.fold_in(key, 11)
    first, second, third, fourth = jax.random.split(key, 4)
    slots = jnp.arange(TILE_DEV * N_ROWS, dtype=jnp.int32)
    owner = slots // TILE_DEV
    nearby = owner * SB_DEV + jax.random.randint(first, slots.shape, 0, SB_DEV)
    anywhere = jax.random.randint(second, slots.shape, 0, BLOCKS)
    coin = jax.random.randint(third, slots.shape, 0, 2)
    target = jnp.where(coin == 1, nearby, anywhere)
    chosen = jax.random.randint(fourth, (), 0, TILE_DEV * N_ROWS)
    target = target.at[chosen].set(BLOCKS - 1)
    return target.astype(jnp.int32)


def draw_tile_count(key, part):
    key = jax.random.fold_in(key, 12)
    first, second = jax.random.split(key, 2)
    level = jax.random.randint(first, (N_ROWS,), 1, 17)
    counts = jnp.maximum(1, level * level * TILE_DEV // 256)
    chosen = jax.random.randint(second, (), 0, N_ROWS)
    counts = counts.at[chosen].set(TILE_DEV)
    return counts.astype(jnp.int32)


def with_ends(result, own_key, least, largest):
    longest = result.shape.index(max(result.shape))
    spots = []
    for shift in (0, 1):
        where = [jax.random.randint(jax.random.fold_in(own_key, axis), (), 0, length) for axis, length in enumerate(result.shape)]
        where[longest] = (where[longest] + shift) % result.shape[longest]
        spots.append(tuple(where))
    return result.at[spots[0]].set(least).at[spots[1]].set(largest)


def shard_levels(stream_key, extent, pieces, low, largest):
    factor_of, own = 1.0, jax.random.fold_in(stream_key, 6)
    for dim, shards_of in pieces:
        heights = jnp.exp(jax.random.uniform(jax.random.fold_in(own, dim), (shards_of,), jnp.float32, low / len(pieces), largest / len(pieces)))
        factor_of = factor_of * jnp.repeat(heights, extent[dim] // shards_of).reshape([-1 if axis == dim else 1 for axis in range(len(extent))])
    return factor_of


def noise(key, dims, width, bound, cuts=(), kind=jnp.bfloat16):
    loudness = shard_levels(key, dims, cuts, -0.22, 0.18) if cuts else 1.0
    array = jax.random.normal(key, dims, jnp.float32) * width * loudness
    return jnp.minimum(jnp.maximum(array, -bound), bound).astype(kind)


def setup_inputs(seed: int = 0, part: int = 0) -> dict:
    splits = jax.random.split(jax.random.key(seed), 9)
    part_splits = jax.random.split(jax.random.fold_in(splits[8], part), 9)
    features = noise(part_splits[0], (F, NODES), 1.0, 6.0, ((0, 4), (1, 4)))
    tile_weights = noise(part_splits[1], (NT, BLK, BLK), (BLK * TPB // 2) ** -0.5, 0.25, ((0, 4),))
    tile_source = with_ends(jax.random.randint(part_splits[2], (NT,), 0, SB_DEV), jax.random.fold_in(part_splits[2], 1), 0, SB_DEV - 1).astype(jnp.int32)
    tile_dest = draw_tile_dest(jax.random.fold_in(jax.random.fold_in(splits[8], part), 71), part)
    tile_count = draw_tile_count(jax.random.fold_in(jax.random.fold_in(splits[8], part), 71), part)
    weight = noise(splits[5], (F, F), F ** -0.5, 0.375)
    bias = noise(splits[6], (F,), 0.5, 3.0)
    cotangent = noise(part_splits[7], (NODES, F), 1.0, 6.0, ((0, 16),))
    return dict(features=features, tile_weights=tile_weights, tile_source=tile_source, tile_dest=tile_dest, tile_count=tile_count, weight=weight, bias=bias, cotangent=cotangent)


def smooth_gate(value):
    return jax.nn.gelu(value, approximate=True)

def reference(features, tile_weights, tile_source, tile_dest, tile_count, weight, bias, cotangent):
    slots = jnp.arange(NT, dtype=jnp.int32)
    owner = slots // TILE_DEV
    live = slots % TILE_DEV < tile_count[owner]
    source = (owner * SB_DEV + tile_source).astype(jnp.int32)
    target = tile_dest.astype(jnp.int32)
    tiles_by_dev = tile_weights.reshape(N_ROWS, TILE_DEV, BLK, BLK)
    source_by_dev = source.reshape(N_ROWS, TILE_DEV)
    target_by_dev = target.reshape(N_ROWS, TILE_DEV)
    live_by_dev = live.reshape(N_ROWS, TILE_DEV)
    feat_blocks = features.astype(jnp.float32).reshape(F, BLOCKS, BLK)

    def forward_dev(total, items):
        tiles_now, source_now, target_now, live_now = items
        picked = jnp.take(feat_blocks, source_now, axis=1)
        product = jnp.einsum('ftj,tij->tfi', picked, tiles_now.astype(jnp.float32))
        product = jnp.where(live_now[:, None, None], product, jnp.float32(0.0))
        return (total.at[target_now].add(product), None)
    start = jnp.zeros((BLOCKS, F, BLK), jnp.float32)
    summed, _ = lax.scan(forward_dev, start, (tiles_by_dev, source_by_dev, target_by_dev, live_by_dev))
    aggregated = jnp.transpose(summed.astype(jnp.bfloat16), (0, 2, 1)).reshape(NODES, F)
    pre = jnp.dot(aggregated, weight, preferred_element_type=jnp.float32) + bias.astype(jnp.float32)
    activated, pullback = jax.vjp(smooth_gate, pre)
    activation = activated.astype(jnp.bfloat16)
    delta = pullback(cotangent.astype(jnp.float32))[0].astype(jnp.bfloat16)
    grad_weight = jnp.dot(aggregated.T, delta, preferred_element_type=jnp.float32)
    grad_bias = lax.optimization_barrier(jnp.sum(delta.astype(jnp.float32), axis=0))
    propagated = jnp.dot(delta, weight.T, preferred_element_type=jnp.float32).astype(jnp.bfloat16)
    prop_blocks = propagated.reshape(BLOCKS, BLK, F)

    def backward_dev(total, items):
        tiles_now, source_now, target_now, live_now = items
        picked = jnp.take(prop_blocks, target_now, axis=0).astype(jnp.float32)
        product = jnp.einsum('tif,tij->tfj', picked, tiles_now.astype(jnp.float32))
        product = jnp.where(live_now[:, None, None], product, jnp.float32(0.0))
        return (total.at[source_now].add(product), None)
    gathered, _ = lax.scan(backward_dev, start, (tiles_by_dev, source_by_dev, target_by_dev, live_by_dev))
    grad_features = jnp.transpose(gathered, (1, 0, 2)).reshape(F, NODES).astype(jnp.bfloat16)
    return (activation, grad_features, grad_weight, grad_bias)
```

```python
import functools
import math

import jax
import jax.numpy as jnp
from jax import lax
from jax.experimental import pallas as pl
from jax.experimental.pallas import tpu as pltpu
from jax.sharding import PartitionSpec as P

BLK = 128
GROUP = 8
RING = 8
VMEM_BYTES = 48 * 1024 * 1024
ROOT = math.sqrt(2.0 / math.pi)
CUBIC = 0.044715
BF16 = jnp.bfloat16
F32 = jnp.float32

SMEM_SPEC = pl.BlockSpec(memory_space=pltpu.SMEM)
VMEM_SPEC = pl.BlockSpec(memory_space=pltpu.VMEM)
ANY_SPEC = pl.BlockSpec(memory_space=pl.ANY)


def bits_of(size):
    return max(1, int(size).bit_length())


def call(body, name, out_shape, in_specs, scratch, flops, nbytes):
    return pl.pallas_call(
        body,
        name=name,
        out_shape=out_shape,
        in_specs=in_specs,
        out_specs=jax.tree.map(lambda _: VMEM_SPEC, out_shape),
        scratch_shapes=scratch,
        compiler_params=pltpu.CompilerParams(vmem_limit_bytes=VMEM_BYTES),
        cost_estimate=pl.CostEstimate(flops=flops, bytes_accessed=nbytes, transcendentals=0),
    )


def each_tile(meta, tiles, picked, ring, sems, tile_bits, dead, multiply, add):
    total = meta.shape[0]
    tile_mask = (1 << tile_bits) - 1

    def scan(step, found):
        for u in range(GROUP):
            entry = meta[step * GROUP + u]
            picked[found] = entry
            found = found + jnp.where(entry >= 0, 1, 0)
        return found

    found = lax.fori_loop(0, total // GROUP, scan, jnp.int32(0))
    for u in range(GROUP):
        picked[found + u] = jnp.int32(dead)
    groups = lax.div(found + (GROUP - 1), GROUP)

    def copies(group):
        base = lax.rem(group, RING) * GROUP
        for u in range(GROUP):
            tile = picked[group * GROUP + u] & tile_mask
            yield pltpu.make_async_copy(tiles.at[tile], ring.at[base + u], sems.at[base + u])

    def start(group, carry):
        for copy in copies(group):
            copy.start()
        return carry

    lax.fori_loop(0, jnp.minimum(groups, RING), start, 0)

    def work(group, carry):
        for copy in copies(group):
            copy.wait()
        base = lax.rem(group, RING) * GROUP
        entries = [picked[group * GROUP + u] >> tile_bits for u in range(GROUP)]
        products = [multiply(entries[u], ring.at[base + u]) for u in range(GROUP)]
        for u in range(GROUP):
            add(entries[u], products[u])

        @pl.when(group + RING < groups)
        def _():
            start(group + RING, 0)

        return carry

    lax.fori_loop(0, groups, work, 0)


def ring_scratch(slots):
    return [
        pltpu.SMEM((slots + GROUP + 1,), jnp.int32),
        pltpu.VMEM((RING * GROUP, BLK, BLK), BF16),
        pltpu.SemaphoreType.DMA((RING * GROUP,)),
    ]


def aggregate(meta, place, tiles, parts, sources, dests, chunk, tile_bits, source_bits, kinds):
    slots = meta.shape[0]
    columns = sum(part.shape[0] for part in parts)
    dead = (dests << source_bits) << tile_bits

    def body(meta_ref, place_ref, tiles_ref, *refs):
        part_refs = refs[: len(parts)]
        outs = refs[len(parts) : len(parts) + len(kinds)]
        turned, total, picked, ring, sems = refs[len(parts) + len(kinds) :]
        for s in range(sources):
            block = jnp.concatenate([ref[:, s * BLK : (s + 1) * BLK] for ref in part_refs], axis=0)
            turned[s] = jnp.transpose(block)
        total[...] = jnp.zeros_like(total)

        def multiply(entry, tile):
            source = entry & ((1 << source_bits) - 1)
            return jnp.dot(tile[...], turned[source], preferred_element_type=F32)

        def add(entry, product):
            total[entry >> source_bits] += product

        each_tile(meta_ref, tiles_ref, picked, ring, sems, tile_bits, dead, multiply, add)
        for i, out in enumerate(outs):
            rows = out.shape[0] // BLK
            out[...] = total[pl.ds(place_ref[i] * chunk, rows)].reshape(out.shape).astype(out.dtype)

    return call(
        body,
        "aggregate",
        [jax.ShapeDtypeStruct((blocks * BLK, columns), kind) for blocks, kind in kinds],
        [SMEM_SPEC, SMEM_SPEC, ANY_SPEC] + [VMEM_SPEC] * len(parts),
        [pltpu.VMEM((sources, BLK, columns), BF16), pltpu.VMEM((dests + 1, BLK, columns), F32)]
        + ring_scratch(slots),
        slots * BLK * BLK * columns,
        slots * BLK * BLK,
    )(meta, place, tiles, *parts)


def spread_back(meta, place, tiles, parts, sources, dests, chunk, tile_bits, source_bits, cols):
    slots = meta.shape[0]
    columns = parts[0].shape[0]
    chips = columns // (2 * cols)
    dead = (dests << source_bits) << tile_bits

    def body(meta_ref, place_ref, tiles_ref, *refs):
        part_refs = refs[: len(parts)]
        keep, send = refs[len(parts) : len(parts) + 2]
        held, total, picked, ring, sems = refs[len(parts) + 2 :]
        held[dests] = jnp.zeros_like(held[dests])
        for i, ref in enumerate(part_refs):
            for q in range(ref.shape[1] // BLK):
                held[place_ref[i] * chunk + q] = ref[:, q * BLK : (q + 1) * BLK]
        total[...] = jnp.zeros_like(total)

        def multiply(entry, tile):
            return jnp.dot(held[entry >> source_bits], tile[...], preferred_element_type=F32)

        def add(entry, product):
            source = entry & ((1 << source_bits) - 1)
            total[source] += product

        each_tile(meta_ref, tiles_ref, picked, ring, sems, tile_bits, dead, multiply, add)
        for s in range(sources):
            for chip in range(chips):
                low = 2 * chip * cols
                spot = (slice(chip * cols, (chip + 1) * cols), slice(s * BLK, (s + 1) * BLK))
                keep[spot] = total[s, low : low + cols, :]
                send[spot] = total[s, low + cols : low + 2 * cols, :].astype(BF16)

    return call(
        body,
        "spread_back",
        [
            jax.ShapeDtypeStruct((chips * cols, sources * BLK), F32),
            jax.ShapeDtypeStruct((chips * cols, sources * BLK), BF16),
        ],
        [SMEM_SPEC, SMEM_SPEC, ANY_SPEC] + [VMEM_SPEC] * len(parts),
        [
            pltpu.VMEM((dests + 2 * chunk, columns, BLK), BF16),
            pltpu.VMEM((sources, columns, BLK), F32),
        ]
        + ring_scratch(slots),
        slots * BLK * BLK * columns,
        slots * BLK * BLK,
    )(meta, place, tiles, *parts)


def layer(spot, near, far, weight, bias, cotangent, cols, chips):
    rows, hidden = cotangent.shape
    near_cols = near[0].shape[1]
    step = 2 * BLK if rows % (2 * BLK) == 0 else BLK
    count = 2 * chips
    lines = cols + 8

    def body(spot_ref, *refs):
        near_refs = refs[: len(near)]
        far_refs = refs[len(near) : len(near) + len(far)]
        weight_ref, bias_ref, cot_ref = refs[len(near) + len(far) : len(near) + len(far) + 3]
        act_ref, near_out, far_out, grad_ref = refs[len(near) + len(far) + 3 :]
        grad_w = [jnp.zeros((near_cols, hidden), F32), jnp.zeros((hidden - near_cols, hidden), F32)]
        grad_b = jnp.zeros((1, hidden), F32)
        for low in range(0, rows, step):
            now = slice(low, low + step)
            mixed = []
            for group in (near_refs, far_refs):
                value = group[0][now, :].astype(F32)
                for ref in group[1:]:
                    value = value + ref[now, :].astype(F32)
                mixed.append(value.astype(BF16))
            pre = jnp.dot(mixed[0], weight_ref[:near_cols, :], preferred_element_type=F32)
            pre = pre + jnp.dot(mixed[1], weight_ref[near_cols:, :], preferred_element_type=F32)
            pre = pre + bias_ref[...].astype(F32)
            square = pre * pre
            bend = jnp.tanh(ROOT * pre * (1.0 + CUBIC * square))
            half = 0.5 * (1.0 + bend)
            act_ref[now, :] = (pre * half).astype(BF16)
            slope = half + 0.5 * ROOT * pre * (1.0 - bend * bend) * (1.0 + 3.0 * CUBIC * square)
            delta = (cot_ref[now, :].astype(F32) * slope).astype(BF16)
            turned = lax.dot_general(
                weight_ref[...], delta, (((1,), (1,)), ((), ())), preferred_element_type=F32
            ).astype(BF16)
            near_out[:, now] = turned[:near_cols, :]
            far_out[:, now] = turned[near_cols:, :]
            for i in range(2):
                grad_w[i] = grad_w[i] + jnp.dot(
                    jnp.transpose(mixed[i]), delta, preferred_element_type=F32
                )
            grad_b = grad_b + jnp.sum(delta.astype(F32), axis=0, keepdims=True)
        tail = jnp.broadcast_to(grad_b, (8, hidden))
        for part in range(count):
            source = grad_w[0] if part < 2 else grad_w[1]
            low = part * cols - (0 if part < 2 else near_cols)
            grad_ref[part % 2, part // 2, :cols, :] = source[low : low + cols, :]
            grad_ref[part % 2, part // 2, cols:, :] = tail

    return call(
        body,
        "layer",
        [
            jax.ShapeDtypeStruct((rows, hidden), BF16),
            jax.ShapeDtypeStruct((near_cols, rows), BF16),
            jax.ShapeDtypeStruct((hidden - near_cols, rows), BF16),
            jax.ShapeDtypeStruct((2, chips, lines, hidden), F32),
        ],
        [SMEM_SPEC] + [VMEM_SPEC] * (len(near) + len(far) + 3),
        [],
        6 * rows * hidden * hidden,
        10 * rows * hidden,
    )(spot, *near, *far, weight, bias, cotangent)


def assemble(spot, mine, other, cols, chips):
    hidden = mine[0].shape[1]

    def body(spot_ref, *refs):
        out, bias_out = refs[-2:]
        chip, core = spot_ref[0], spot_ref[1]
        for k, group in enumerate((refs[:chips], refs[chips : 2 * chips])):
            for s in range(chips):
                owner = lax.rem(chip + s, chips) * 2 + (core if k == 0 else 1 - core)
                low = pl.multiple_of(owner * cols, cols)
                out[pl.ds(low, cols), :] = group[s][:cols, :]
        bias_out[...] = refs[0][cols : cols + 1, :]

    return call(
        body,
        "assemble",
        [
            jax.ShapeDtypeStruct((2 * chips * cols, hidden), F32),
            jax.ShapeDtypeStruct((1, hidden), F32),
        ],
        [SMEM_SPEC] + [VMEM_SPEC] * (2 * chips),
        [],
        0,
        8 * chips * cols * hidden,
    )(spot, *mine, *other)


def per_device(features, tile_weights, tile_source, tile_dest, tile_count, weight, bias, cotangent):
    cols, width = features.shape
    sources = width // BLK
    slots = tile_weights.shape[0]
    hidden = weight.shape[0]
    wide = lax.axis_size("wide")
    chips = wide // 2
    n_rows = lax.axis_size("rows")
    chunk = sources // wide
    dests = n_rows * chunk
    relay = n_rows == 4
    tile_bits, source_bits = bits_of(slots), bits_of(sources)

    at = lax.axis_index("wide")
    chip, core = at // 2, at % 2
    row = lax.axis_index("rows")

    def swap_cores(value):
        return lax.ppermute(value, "wide", [(i, i ^ 1) for i in range(wide)])

    def from_chip(value, shift):
        pairs = [(2 * ((i + shift) % chips) + k, 2 * i + k) for i in range(chips) for k in range(2)]
        return lax.ppermute(value, "wide", pairs)

    def along(value, pairs):
        return lax.ppermute(value, "rows", pairs)

    up, down = [(0, 1), (1, 2), (2, 3)], [(1, 0), (2, 1), (3, 2)]
    skip = [(0, 2), (1, 3), (2, 0), (3, 1)]

    slot = jnp.arange(slots, dtype=jnp.int32)
    within = tile_dest % sources
    mine = (slot < tile_count[0]) & (within // chunk == at)
    index = (tile_dest // sources) * chunk + within % chunk
    meta = jnp.where(mine, (index << (source_bits + tile_bits)) | (tile_source << tile_bits) | slot, -1)

    distant = [from_chip(features, s) for s in range(1, chips)]
    near_parts = [features, swap_cores(features)]

    if relay:
        last = n_rows - 1
        out_place = jnp.stack(
            [row, jnp.minimum(row + 1, last), jnp.maximum(row - 1, 0), row ^ 2, last - row]
        ).astype(jnp.int32)
        kinds = [(chunk, F32)] + [(chunk, BF16)] * 4
    else:
        out_place = jnp.zeros((1,), jnp.int32)
        kinds = [(dests, BF16)]

    def summed(parts):
        outs = aggregate(
            meta, out_place, tile_weights, parts, sources, dests, chunk, tile_bits, source_bits, kinds
        )
        if not relay:
            return [lax.psum_scatter(outs[0], "rows", scatter_dimension=0, tiled=True)]
        own, to_up, to_down, to_skip, ends = outs
        passed = along(ends, [(0, 1), (3, 2)])
        got_up = along(to_up, up)
        got_down = along(to_down, down)
        got_skip = along((to_skip.astype(F32) + passed.astype(F32)).astype(BF16), skip)
        return [own, got_up, got_down, got_skip]

    near = summed(near_parts)
    far_parts = []
    for value in distant:
        far_parts += [value, swap_cores(value)]
    far = summed(far_parts)

    order = (2 * ((chip + jnp.arange(chips)) % chips))[:, None] + (core ^ jnp.arange(2))[None, :]
    ordered = jnp.take(weight.reshape(wide, cols, hidden), order.reshape(-1), axis=0)
    spot = jnp.stack([chip, core]).astype(jnp.int32)
    activation, near_prop, far_prop, grads = layer(
        spot, near, far, ordered.reshape(hidden, hidden), bias.reshape(1, hidden), cotangent, cols, chips
    )

    if relay:
        in_place = jnp.stack(
            [
                row,
                jnp.where(row > 0, row - 1, n_rows),
                jnp.where(row < last, row + 1, n_rows),
                row ^ 2,
                jnp.where(row == 0, last, jnp.where(row == last, 0, n_rows)),
            ]
        ).astype(jnp.int32)
    else:
        in_place = jnp.zeros((1,), jnp.int32)

    def gathered(value):
        if not relay:
            return [lax.all_gather(value, "rows", axis=1, tiled=True)]
        got_skip = along(value, skip)
        got_up = along(value, up)
        got_down = along(value, down)
        got_ends = along(got_skip, [(2, 3), (1, 0)])
        return [value, got_up, got_down, got_skip, got_ends]

    def back(value):
        return spread_back(
            meta, in_place, tile_weights, gathered(value), sources, dests, chunk, tile_bits, source_bits, cols
        )

    far_keep, far_send = back(far_prop)
    far_sum = (far_keep + swap_cores(far_send).astype(F32)).astype(BF16)
    arrived = [
        from_chip(far_sum[(chips - s - 1) * cols : (chips - s) * cols], s) for s in range(1, chips)
    ]

    part = grads[0] + swap_cores(grads[1])
    quarter = part[0]
    for s in range(1, chips):
        quarter = quarter + from_chip(part[chips - s], s)
    if relay:
        quarter = quarter + along(quarter, [(0, 1), (1, 0), (2, 3), (3, 2)])
        quarter = quarter + along(quarter, skip)
    else:
        quarter = lax.psum(quarter, "rows")
    half = [quarter] + [from_chip(quarter, s) for s in range(1, chips)]
    whole_half = jnp.stack(half)
    other_half = swap_cores(whole_half)
    grad_weight, grad_bias = assemble(
        spot, half, [other_half[s] for s in range(chips)], cols, chips
    )

    near_keep, near_send = back(near_prop)
    total = near_keep + swap_cores(near_send).astype(F32)
    for value in arrived:
        total = total + value.astype(F32)
    grad_features = total.astype(BF16)
    return (activation, grad_features, grad_weight, grad_bias.reshape(hidden))


def solution(mesh):
    in_specs = (
        P("wide", ("groups", "rows")),
        P(("groups", "rows"), None, None),
        P(("groups", "rows")),
        P(("groups", "rows")),
        P(("groups", "rows")),
        P(),
        P(),
        P(("groups", "rows", "wide"), None),
    )
    out_specs = (
        P(("groups", "rows", "wide"), None),
        P("wide", ("groups", "rows")),
        P("groups", None),
        P("groups"),
    )
    return jax.shard_map(
        per_device, mesh=mesh, in_specs=in_specs, out_specs=out_specs, check_vma=False
    )
```

```python
import functools
import math

import jax
import jax.numpy as jnp
from jax import lax
from jax.experimental import pallas as pl
from jax.experimental.pallas import tpu as pltpu
from jax.sharding import PartitionSpec as P

BLK = 128
GROUP = 16
RS_FAR = "pair"
RS_NEAR = "pair"
AG_NEAR = "pair"
AG_FAR = "all"
TIE = 0
RING = 4
VMEM_BYTES = 48 * 1024 * 1024
ROOT = math.sqrt(2.0 / math.pi)
CUBIC = 0.044715
BF16 = jnp.bfloat16
F32 = jnp.float32

SMEM_SPEC = pl.BlockSpec(memory_space=pltpu.SMEM)
VMEM_SPEC = pl.BlockSpec(memory_space=pltpu.VMEM)
ANY_SPEC = pl.BlockSpec(memory_space=pl.ANY)


def bits_of(size):
    return max(1, int(size).bit_length())


def call(body, name, out_shape, in_specs, scratch, flops, nbytes):
    return pl.pallas_call(
        body,
        name=name,
        out_shape=out_shape,
        in_specs=in_specs,
        out_specs=jax.tree.map(lambda _: VMEM_SPEC, out_shape),
        scratch_shapes=scratch,
        compiler_params=pltpu.CompilerParams(vmem_limit_bytes=VMEM_BYTES),
        cost_estimate=pl.CostEstimate(flops=flops, bytes_accessed=nbytes, transcendentals=0),
    )


def each_tile(meta, wanted, picked, tiles, ring, sems, tile_bits, prepare, multiply, add):
    total = meta.shape[0]
    tile_mask = (1 << tile_bits) - 1

    def scan(step, found):
        for u in range(GROUP):
            entry = meta[step * GROUP + u]
            picked[found] = entry
            found = found + jnp.where(wanted(entry), 1, 0)
        return found

    found = lax.fori_loop(0, total // GROUP, scan, jnp.int32(0))
    for u in range(GROUP):
        picked[found + u] = jnp.int32(-1)
    groups = lax.div(found + (GROUP - 1), GROUP)

    def copies(group):
        base = lax.rem(group, RING) * GROUP
        for u in range(GROUP):
            tile = jnp.maximum(picked[group * GROUP + u], 0) & tile_mask
            yield pltpu.make_async_copy(tiles.at[tile], ring.at[base + u], sems.at[base + u])

    def start(group, carry):
        for copy in copies(group):
            copy.start()
        return carry

    lax.fori_loop(0, jnp.minimum(groups, RING), start, 0)
    prepare()

    def work(group, carry):
        for copy in copies(group):
            copy.wait()
        base = lax.rem(group, RING) * GROUP
        entries = [picked[group * GROUP + u] for u in range(GROUP)]
        products = [multiply(entries[u], ring.at[base + u]) for u in range(GROUP)]
        for u in range(GROUP):
            add(entries[u], products[u])

        @pl.when(group + RING < groups)
        def _():
            start(group + RING, 0)

        return carry

    lax.fori_loop(0, groups, work, 0)


def ring_scratch(slots):
    return [
        pltpu.SMEM((slots + GROUP,), jnp.int32),
        pltpu.VMEM((RING * GROUP, BLK, BLK), BF16),
        pltpu.SemaphoreType.DMA((RING * GROUP,)),
    ]


def row_at(shift):
    count = lax.axis_size("rows")
    return lax.rem(lax.axis_index("rows") + (shift % count), count)


def places_of(way, scatter):
    count = lax.axis_size("rows")
    if way == "all":
        return [(row, True) for row in range(count)]
    if way == "direct":
        return [(row_at(s if scatter else -s), True) for s in range(count)]
    row = lax.axis_index("rows")
    if scatter:
        return [(row ^ i, True) for i in (0, 3, 1, 2)]
    return [(row ^ i, True) for i in (0, 2, 1, 3)]


def aggregate(meta, tiles, parts, first, dests, chunk, tile_bits, source_bits, way):
    columns = sum(part.shape[0] for part in parts)
    sources = parts[0].shape[1] // BLK
    source_mask = (1 << source_bits) - 1
    if way == "all":
        shapes = [jax.ShapeDtypeStruct((dests * BLK, columns), BF16)]
    else:
        count = dests // chunk
        shapes = [
            jax.ShapeDtypeStruct((chunk * BLK, columns), F32 if i == 0 else BF16) for i in range(count)
        ]

    def body(meta_ref, tiles_ref, own_ref, *refs):
        part_refs = refs[: len(parts) - 1]
        outs = refs[len(parts) - 1 : len(parts) - 1 + len(shapes)]
        own, own_sem, turned, total, picked, ring, sems = refs[len(parts) - 1 + len(shapes) :]
        fetch = pltpu.make_async_copy(own_ref, own, own_sem)
        fetch.start()

        def prepare():
            fetch.wait()
            total[...] = jnp.zeros_like(total)
            for s in range(sources):
                now = slice(s * BLK, (s + 1) * BLK)
                block = jnp.concatenate([own[:, now]] + [ref[:, now] for ref in part_refs], axis=0)
                turned[s] = jnp.transpose(block)

        def multiply(entry, tile):
            source = (jnp.maximum(entry, 0) >> tile_bits) & source_mask
            return jnp.dot(tile[...], turned[source], preferred_element_type=F32)

        def add(entry, product):
            dest = (entry >> (tile_bits + source_bits)) - first
            total[jnp.where(entry < 0, dests, dest)] += product

        def wanted(entry):
            dest = entry >> (tile_bits + source_bits)
            return (dest >= first) & (dest < first + dests)

        each_tile(
            meta_ref, wanted, picked, tiles_ref, ring, sems, tile_bits, prepare, multiply, add
        )
        if way == "all":
            outs[0][...] = total[:dests].reshape(outs[0].shape).astype(BF16)
        else:
            for out, (place, _) in zip(outs, places_of(way, True)):
                out[...] = total[pl.ds(place * chunk, chunk)].reshape(out.shape).astype(out.dtype)

    slots = tiles.shape[0]
    return call(
        body,
        "aggregate",
        shapes,
        [SMEM_SPEC, ANY_SPEC, ANY_SPEC] + [VMEM_SPEC] * (len(parts) - 1),
        [
            pltpu.VMEM(parts[0].shape, BF16),
            pltpu.SemaphoreType.DMA,
            pltpu.VMEM((sources, BLK, columns), BF16),
            pltpu.VMEM((dests + 1, BLK, columns), F32),
        ]
        + ring_scratch(tiles.shape[0]),
        slots * BLK * BLK * columns,
        slots * BLK * BLK,
    )(meta, tiles, *parts)


def spread_back(meta, tiles, groups, columns, sources, tile_bits, source_bits, cols):
    source_mask = (1 << source_bits) - 1
    given = [piece for _, _, pieces in groups for piece in pieces]
    sizes = [blocks * lax.axis_size("rows") for blocks, _, _ in groups]
    spare = sum(sizes)

    def body(meta_ref, tiles_ref, *refs):
        part_refs = refs[: len(given)]
        keep, send, held, total, picked, ring, sems = refs[len(given) :]

        def prepare():
            total[...] = jnp.zeros_like(total)
            held[spare] = jnp.zeros_like(held[spare])
            start, at = 0, 0
            for (blocks, way, pieces), size in zip(groups, sizes):
                places = places_of(way, False)
                count = len(places) // len(pieces)
                for i, (place, there) in enumerate(places):
                    ref = part_refs[at + i // count]
                    low = (i % count) * (ref.shape[0] // count)

                    def take(ref=ref, low=low, place=place, blocks=blocks, start=start):
                        for q in range(blocks):
                            held[start + place * blocks + q] = ref[
                                low : low + columns, q * BLK : (q + 1) * BLK
                            ]

                    if there is True:
                        take()
                    else:
                        pl.when(there)(take)
                at += len(pieces)
                start += size

        def multiply(entry, tile):
            dest = jnp.where(entry < 0, spare, entry >> (tile_bits + source_bits))
            return jnp.dot(held[dest], tile[...], preferred_element_type=F32)

        def add(entry, product):
            source = (jnp.maximum(entry, 0) >> tile_bits) & source_mask
            total[source] += product

        each_tile(
            meta_ref, lambda entry: entry >= 0, picked, tiles_ref, ring, sems, tile_bits,
            prepare, multiply, add,
        )
        for s in range(sources):
            keep[:, s * BLK : (s + 1) * BLK] = total[s, :cols, :]
            send[:, s * BLK : (s + 1) * BLK] = total[s, cols:, :].astype(BF16)

    slots = tiles.shape[0]
    return call(
        body,
        "spread_back",
        [
            jax.ShapeDtypeStruct((cols, sources * BLK), F32),
            jax.ShapeDtypeStruct((cols, sources * BLK), BF16),
        ],
        [SMEM_SPEC, ANY_SPEC] + [VMEM_SPEC] * len(given),
        [
            pltpu.VMEM((spare + 1, columns, BLK), BF16),
            pltpu.VMEM((sources, columns, BLK), F32),
        ]
        + ring_scratch(tiles.shape[0]),
        slots * BLK * BLK * columns,
        slots * BLK * BLK,
    )(meta, tiles, *given)


def spot_order(chips):
    at = lax.axis_index("wide")
    chip, core = at >> 1, at & 1
    return [
        2 * lax.rem(chip + s, chips) + (core if k == 0 else 1 - core) for s in range(chips) for k in range(2)
    ]


def layer(near, far, weight, bias, cotangent, cols, chips):
    rows, hidden = cotangent.shape
    near_cols = near[0].shape[1]
    step = 2 * BLK if rows % (2 * BLK) == 0 else BLK

    def body(*refs):
        near_refs = refs[: len(near)]
        far_refs = refs[len(near) : len(near) + len(far)]
        weight_ref, bias_ref, cot_ref = refs[len(near) + len(far) : len(near) + len(far) + 3]
        act_ref, near_out, far_out, near_mix, far_mix, delta_ref, ordered = refs[
            len(near) + len(far) + 3 :
        ]
        for part, owner in enumerate(spot_order(chips)):
            low = pl.multiple_of(owner * cols, cols)
            ordered[part * cols : (part + 1) * cols, :] = weight_ref[pl.ds(low, cols), :]
        for low in range(0, rows, step):
            now = slice(low, low + step)
            mixed = []
            for group, out in ((near_refs, near_mix), (far_refs, far_mix)):
                value = group[0][now, :].astype(F32)
                for ref in group[1:]:
                    value = value + ref[now, :].astype(F32)
                mixed.append(value.astype(BF16))
                out[now, :] = mixed[-1]
            pre = jnp.dot(mixed[0], ordered[:near_cols, :], preferred_element_type=F32)
            pre = pre + jnp.dot(mixed[1], ordered[near_cols:, :], preferred_element_type=F32)
            pre = pre + bias_ref[...].astype(F32)
            square = pre * pre
            bend = jnp.tanh(ROOT * pre * (1.0 + CUBIC * square))
            half = 0.5 * (1.0 + bend)
            act_ref[now, :] = (pre * half).astype(BF16)
            slope = half + 0.5 * ROOT * pre * (1.0 - bend * bend) * (1.0 + 3.0 * CUBIC * square)
            delta = (cot_ref[now, :].astype(F32) * slope).astype(BF16)
            delta_ref[now, :] = delta
            turned = lax.dot_general(
                ordered[...], delta, (((1,), (1,)), ((), ())), preferred_element_type=F32
            ).astype(BF16)
            near_out[:, now] = turned[:near_cols, :]
            far_out[:, now] = turned[near_cols:, :]

    return call(
        body,
        "layer",
        [
            jax.ShapeDtypeStruct((rows, hidden), BF16),
            jax.ShapeDtypeStruct((near_cols, rows), BF16),
            jax.ShapeDtypeStruct((hidden - near_cols, rows), BF16),
            jax.ShapeDtypeStruct((rows, near_cols), BF16),
            jax.ShapeDtypeStruct((rows, hidden - near_cols), BF16),
            jax.ShapeDtypeStruct((rows, hidden), BF16),
        ],
        [VMEM_SPEC] * (len(near) + len(far) + 3),
        [pltpu.VMEM((hidden, hidden), BF16)],
        4 * rows * hidden * hidden,
        10 * rows * hidden,
    )(*near, *far, weight, bias, cotangent)


def weight_parts(near_mix, far_mix, delta, cols, chips):
    rows, near_cols = near_mix.shape
    hidden = delta.shape[1]
    lines = cols + 8

    def body(near_ref, far_ref, delta_ref, grad_ref):
        tail = jnp.broadcast_to(
            jnp.sum(delta_ref[...].astype(F32), axis=0, keepdims=True), (8, hidden)
        )
        grads = [
            lax.dot_general(
                ref[...], delta_ref[...], (((0,), (0,)), ((), ())), preferred_element_type=F32
            )
            for ref in (near_ref, far_ref)
        ]
        for part in range(2 * chips):
            source = grads[0] if part < 2 else grads[1]
            low = part * cols - (0 if part < 2 else near_cols)
            grad_ref[part % 2, part // 2, :cols, :] = source[low : low + cols, :]
            grad_ref[part % 2, part // 2, cols:, :] = tail

    return call(
        body,
        "weight_parts",
        [jax.ShapeDtypeStruct((2, chips, lines, hidden), F32)],
        [VMEM_SPEC] * 3,
        [],
        2 * rows * hidden * hidden,
        6 * rows * hidden,
    )(near_mix, far_mix, delta)[0]


def weight_sums(way, pieces, top, lines, packed, hidden):
    n_rows = lax.axis_size("rows")
    width = pieces[0].shape[1] // hidden

    def body(*refs):
        out, held = refs[-2:]
        places = places_of(way, False)
        count = len(places) // len(pieces)
        for i, (place, there) in enumerate(places):
            ref = refs[i // count]
            low = (i % count) * (ref.shape[0] // count) + top

            def take(ref=ref, low=low, place=place):
                for k in range(width):
                    rows = min(packed, lines - k * packed)
                    if rows > 0:
                        part = ref[low : low + packed, k * hidden : (k + 1) * hidden].astype(F32)
                        held[place, k * packed : k * packed + rows, :] = part[:rows]

            if there is True:
                take()
            else:
                pl.when(there)(take)
        value = held[0]
        for r in range(1, n_rows):
            value = value + held[r]
        out[...] = value

    return call(
        body,
        "weight_sums",
        [jax.ShapeDtypeStruct((lines, hidden), F32)],
        [VMEM_SPEC] * len(pieces),
        [pltpu.VMEM((n_rows, lines, hidden), F32)],
        0,
        8 * lines * hidden,
    )(*pieces)[0]


def assemble(mine, other, cols, chips):
    hidden = mine[0].shape[1]

    def body(*refs):
        out, bias_out = refs[-2:]
        for part, owner in enumerate(spot_order(chips)):
            low = pl.multiple_of(owner * cols, cols)
            out[pl.ds(low, cols), :] = refs[(part % 2) * chips + part // 2][:cols, :]
        bias_out[...] = refs[0][cols : cols + 1, :]

    return call(
        body,
        "assemble",
        [
            jax.ShapeDtypeStruct((2 * chips * cols, hidden), F32),
            jax.ShapeDtypeStruct((1, hidden), F32),
        ],
        [VMEM_SPEC] * (2 * chips),
        [],
        0,
        8 * chips * cols * hidden,
    )(*mine, *other)


def per_device(features, tile_weights, tile_source, tile_dest, tile_count, weight, bias, cotangent):
    cols, width = features.shape
    sources = width // BLK
    slots = tile_weights.shape[0]
    hidden = weight.shape[0]
    wide = lax.axis_size("wide")
    chips = wide // 2
    n_rows = lax.axis_size("rows")
    chunk = sources // wide
    near_cols = 2 * cols
    lines = cols + 8
    tile_bits, source_bits = bits_of(slots), bits_of(sources)

    at = lax.axis_index("wide")
    chip, core = at >> 1, at & 1

    def swap_cores(value):
        return lax.ppermute(value, "wide", [(i, i ^ 1) for i in range(wide)])

    def from_chip(value, shift):
        pairs = [(2 * ((i + shift) % chips) + k, 2 * i + k) for i in range(chips) for k in range(2)]
        return lax.ppermute(value, "wide", pairs)

    def along(value, pairs):
        return lax.ppermute(value, "rows", pairs)

    def around(value, shift):
        return along(value, [(i, (i + shift) % n_rows) for i in range(n_rows)])

    beside, across_pairs = [(0, 1), (1, 0), (2, 3), (3, 2)], [(0, 2), (1, 3), (2, 0), (3, 1)]

    def known(way):
        return way if n_rows == 4 or way == "all" else "direct"

    def scattered(way, first, blocks):
        outs = aggregate(
            meta, tile_weights, parts, first, n_rows * blocks, blocks, tile_bits, source_bits, way
        )
        if way == "direct":
            return [outs[0]] + [around(outs[s], s) for s in range(1, n_rows)]
        own, to_far, to_next, to_skip = outs
        passed = along(to_far, beside)
        got_next = along(to_next, beside)
        merged = (to_skip.astype(F32) + passed.astype(F32)).astype(BF16)
        got_skip = along(merged, across_pairs)
        return [own, got_next, got_skip]

    def gathered(way, value):
        if way == "all":
            return [lax.all_gather(value, "rows", axis=0, tiled=True)]
        if way == "direct":
            return [value] + [around(value, s) for s in range(1, n_rows)]
        got_skip = along(value, across_pairs)
        got_next = along(value, beside)
        return [value, got_skip, got_next, along(got_skip, beside)]

    parts = [features, swap_cores(features)]

    def split(value, size):
        whole = ((value.astype(F32) + 0.5) * (1.0 / size)).astype(jnp.int32)
        return whole, value - whole * size

    slot = jnp.arange(slots, dtype=jnp.int32)
    owner, within = split(tile_dest, sources)
    holder, nth = split(within, chunk)
    away = (holder >> 1) - chip
    away = jnp.where(away < 0, away + chips, away)
    far_blocks = (chips - 1) * chunk
    first_far = n_rows * chunk
    index = jnp.where(
        away == 0, owner * chunk + nth, first_far + owner * far_blocks + (away - 1) * chunk + nth
    )
    ours = (slot < tile_count[0]) & ((holder & 1) == core)
    high = source_bits + tile_bits
    meta = jnp.where(ours, (index << high) | (tile_source << tile_bits) | slot, -1)

    far_terms = scattered(known(RS_FAR), first_far, far_blocks)
    near = scattered(known(RS_NEAR), 0, chunk)
    passing = far_terms[0]
    for term in far_terms[1:]:
        passing = passing + term.astype(F32)
    passing = passing.astype(BF16).reshape(chips - 1, chunk * BLK, near_cols)
    far = [from_chip(passing[chips - s - 1], s) for s in range(1, chips)]
    far = far[0] if chips == 2 else jnp.concatenate(far, axis=1)

    activation, near_prop, far_prop, near_mix, far_mix, delta = layer(
        near, [far], weight, bias.reshape(1, hidden), cotangent, cols, chips
    )

    far_prop = far_prop.reshape(chips - 1, near_cols, chunk * BLK)
    coming = [from_chip(far_prop[chips - s - 1], s) for s in range(1, chips)]
    coming = coming[0] if chips == 2 else jnp.concatenate(coming, axis=1)
    near_all = gathered(known(AG_NEAR), near_prop)

    grads = weight_parts(near_mix, far_mix, delta, cols, chips)
    part = grads[0] + swap_cores(grads[1])
    quarter = part[0]
    for s in range(1, chips):
        quarter = quarter + from_chip(part[chips - s], s)
    across = coming.shape[1] // hidden
    packed = -(-lines // across)
    extra = jnp.pad(quarter.astype(BF16), ((0, across * packed - lines), (0, 0)))
    extra = jnp.concatenate([extra[k * packed : (k + 1) * packed] for k in range(across)], axis=1)
    spare = -(-packed // 16) * 16
    extra = jnp.pad(extra, ((0, spare - packed), (0, 0)))
    payload = jnp.concatenate([coming, extra], axis=0)
    if TIE == 1:
        payload = lax.optimization_barrier((payload, near_all[1]))[0]
    elif TIE == 2:
        payload = lax.optimization_barrier((payload, near_all[1:3]))[0]
    elif TIE == 3:
        payload = lax.optimization_barrier((payload, near_all[1:4]))[0]
    far_all = gathered(known(AG_FAR), payload)

    keep, send = spread_back(
        meta, tile_weights,
        [(chunk, known(AG_NEAR), near_all), (far_blocks, known(AG_FAR), far_all)],
        near_cols, sources, tile_bits, source_bits, cols,
    )
    grad_features = (keep + swap_cores(send).astype(F32)).astype(BF16)

    quarter = weight_sums(known(AG_FAR), far_all, near_cols, lines, packed, hidden)
    half = [quarter] + [from_chip(quarter, s) for s in range(1, chips)]
    other_half = swap_cores(jnp.stack(half))
    grad_weight, grad_bias = assemble(half, [other_half[s] for s in range(chips)], cols, chips)
    return (activation, grad_features, grad_weight, grad_bias.reshape(hidden))


def solution(mesh):
    in_specs = (
        P("wide", ("groups", "rows")),
        P(("groups", "rows"), None, None),
        P(("groups", "rows")),
        P(("groups", "rows")),
        P(("groups", "rows")),
        P(),
        P(),
        P(("groups", "rows", "wide"), None),
    )
    out_specs = (
        P(("groups", "rows", "wide"), None),
        P("wide", ("groups", "rows")),
        P("groups", None),
        P("groups"),
    )
    return jax.shard_map(
        per_device, mesh=mesh, in_specs=in_specs, out_specs=out_specs, check_vma=False
    )
```

```python
import functools
import math

import jax
import jax.numpy as jnp
from jax import lax
from jax.experimental import pallas as pl
from jax.experimental.pallas import tpu as pltpu
from jax.sharding import PartitionSpec as P

BLK = 128
GROUP = 16
AG_NEAR = "pair"
AG_FAR = 'all'
TIE = 0
QTIE = 0
COST = 1
XG = False
SPLIT = False
RING = 4
VMEM_BYTES = 48 * 1024 * 1024
ROOT = math.sqrt(2.0 / math.pi)
CUBIC = 0.044715
BF16 = jnp.bfloat16
F32 = jnp.float32

SMEM_SPEC = pl.BlockSpec(memory_space=pltpu.SMEM)
VMEM_SPEC = pl.BlockSpec(memory_space=pltpu.VMEM)
HBM_SPEC = pl.BlockSpec(memory_space=pltpu.HBM)


def bits_of(size):
    return max(1, int(size).bit_length())


def call(body, name, out_shape, in_specs, scratch, flops, nbytes):
    return pl.pallas_call(
        body,
        name=name,
        out_shape=out_shape,
        in_specs=in_specs,
        out_specs=jax.tree.map(lambda _: VMEM_SPEC, out_shape),
        scratch_shapes=scratch,
        compiler_params=pltpu.CompilerParams(vmem_limit_bytes=VMEM_BYTES),
        cost_estimate=pl.CostEstimate(flops=COST * flops, bytes_accessed=COST * nbytes, transcendentals=0),
    )


def each_tile(meta, wanted, picked, tiles, ring, sems, tile_bits, prepare, multiply, add):
    total = meta.shape[0]
    tile_mask = (1 << tile_bits) - 1

    def scan(step, found):
        for u in range(GROUP):
            entry = meta[step * GROUP + u]
            picked[found] = entry
            found = found + jnp.where(wanted(entry), 1, 0)
        return found

    found = lax.fori_loop(0, total // GROUP, scan, jnp.int32(0))
    for u in range(GROUP):
        picked[found + u] = jnp.int32(-1)
    groups = lax.div(found + (GROUP - 1), GROUP)

    def copies(group):
        base = lax.rem(group, RING) * GROUP
        for u in range(GROUP):
            tile = jnp.maximum(picked[group * GROUP + u], 0) & tile_mask
            yield pltpu.make_async_copy(tiles.at[tile], ring.at[base + u], sems.at[base + u])

    def start(group, carry):
        for copy in copies(group):
            copy.start()
        return carry

    lax.fori_loop(0, jnp.minimum(groups, RING), start, 0)
    prepare()

    def work(group, carry):
        for copy in copies(group):
            copy.wait()
        base = lax.rem(group, RING) * GROUP
        entries = [picked[group * GROUP + u] for u in range(GROUP)]
        products = [multiply(entries[u], ring.at[base + u]) for u in range(GROUP)]
        for u in range(GROUP):
            add(entries[u], products[u])

        @pl.when(group + RING < groups)
        def _():
            start(group + RING, 0)

        return carry

    lax.fori_loop(0, groups, work, 0)


def ring_scratch(slots):
    return [
        pltpu.SMEM((slots + GROUP,), jnp.int32),
        pltpu.VMEM((RING * GROUP, BLK, BLK), BF16),
        pltpu.SemaphoreType.DMA((RING * GROUP,)),
    ]


def row_at(way, i):
    count = lax.axis_size("rows")
    row = lax.axis_index("rows")
    if way == "all":
        return i
    if way == "direct":
        return lax.rem(row + (i % count), count)
    return row ^ i


def aggregate(meta, tiles, parts, owners, way, cuts, layout):
    tile_bits, source_bits, nth_bits = layout
    columns = sum(part.shape[0] for part in parts)
    sources = parts[0].shape[1] // BLK
    n_rows, per_row = lax.axis_size("rows"), cuts[-1]
    dead = n_rows * per_row
    pieces = list(zip(cuts[:-1], cuts[1:]))
    shapes = [
        jax.ShapeDtypeStruct(((high - low) * BLK, columns), F32 if i == 0 else BF16)
        for i in owners
        for low, high in pieces
    ]
    many = len(owners) == n_rows

    def body(meta_ref, tiles_ref, own_ref, *refs):
        part_refs = refs[: len(parts) - 1]
        outs = refs[len(parts) - 1 : len(parts) - 1 + len(shapes)]
        own, own_sem, turned, total, picked, ring, sems = refs[len(parts) - 1 + len(shapes) :]
        fetch = pltpu.make_async_copy(own_ref, own, own_sem)
        fetch.start()
        rows = [row_at(way, i) for i in owners]

        def prepare():
            fetch.wait()
            if many:
                total[...] = jnp.zeros_like(total)
            else:
                total[dead] = jnp.zeros_like(total[dead])
                for row in rows:
                    total[pl.ds(row * per_row, per_row)] = jnp.zeros((per_row, BLK, columns), F32)
            for s in range(sources):
                now = slice(s * BLK, (s + 1) * BLK)
                block = jnp.concatenate([own[:, now]] + [ref[:, now] for ref in part_refs], axis=0)
                turned[s] = jnp.transpose(block)

        def multiply(entry, tile):
            source = (jnp.maximum(entry, 0) >> tile_bits) & ((1 << source_bits) - 1)
            return jnp.dot(tile[...], turned[source], preferred_element_type=F32)

        def add(entry, product):
            rest = entry >> (tile_bits + source_bits)
            dest = (rest >> nth_bits) * per_row + (rest & ((1 << nth_bits) - 1))
            total[jnp.where(entry < 0, dead, dest)] += product

        def wanted(entry):
            if many:
                return entry >= 0
            owner = entry >> (tile_bits + source_bits + nth_bits)
            found = owner == rows[0]
            for row in rows[1:]:
                found = found | (owner == row)
            return found

        each_tile(
            meta_ref, wanted, picked, tiles_ref, ring, sems, tile_bits, prepare, multiply, add
        )
        spots = [(row * per_row + low, high - low) for row in rows for low, high in pieces]
        for out, (low, count) in zip(outs, spots):
            out[...] = total[pl.ds(low, count)].reshape(out.shape).astype(out.dtype)

    slots = tiles.shape[0]
    return call(
        body,
        "aggregate",
        shapes,
        [SMEM_SPEC, HBM_SPEC, HBM_SPEC] + [VMEM_SPEC] * (len(parts) - 1),
        [
            pltpu.VMEM(parts[0].shape, BF16),
            pltpu.SemaphoreType.DMA,
            pltpu.VMEM((sources, BLK, columns), BF16),
            pltpu.VMEM((dead + 1, BLK, columns), F32),
        ]
        + ring_scratch(tiles.shape[0]),
        slots * BLK * BLK * columns,
        slots * BLK * BLK,
    )(meta, tiles, *parts)


def spread_back(meta, tiles, pieces, before, columns, sources, per_row, layout, cols, last):
    tile_bits, source_bits, nth_bits = layout
    given = []
    for piece in pieces:
        if not any(piece[0] is other for other in given):
            given.append(piece[0])
    extra = [] if before is None else [before]
    spare = lax.axis_size("rows") * per_row

    def body(meta_ref, tiles_ref, *refs):
        rest = refs[len(given) + len(extra) :]
        if last:
            keep, send, held, total, picked, ring, sems = rest
        else:
            total, held, picked, ring, sems = rest
        rows = [row_at(way, i) for _, _, way, i, _, _ in pieces]

        def prepare():
            if before is None:
                total[...] = jnp.zeros_like(total)
            else:
                total[...] = refs[len(given)][...]
            held[spare] = jnp.zeros_like(held[spare])
            for (array, line, _, _, first, count), row in zip(pieces, rows):
                ref = next(ref for ref, other in zip(refs, given) if other is array)
                for q in range(count):
                    held[row * per_row + first + q] = ref[
                        line : line + columns, q * BLK : (q + 1) * BLK
                    ]

        def wanted(entry):
            rest = entry >> (tile_bits + source_bits)
            owner, nth = rest >> nth_bits, rest & ((1 << nth_bits) - 1)
            found = owner < 0
            for (_, _, _, _, first, count), row in zip(pieces, rows):
                found = found | ((owner == row) & (nth >= first) & (nth < first + count))
            return found & (entry >= 0)

        def multiply(entry, tile):
            rest = entry >> (tile_bits + source_bits)
            dest = (rest >> nth_bits) * per_row + (rest & ((1 << nth_bits) - 1))
            dest = jnp.where(entry < 0, spare, dest)
            return jnp.dot(held[dest], tile[...], preferred_element_type=F32)

        def add(entry, product):
            source = (jnp.maximum(entry, 0) >> tile_bits) & ((1 << source_bits) - 1)
            total[source] += product

        each_tile(
            meta_ref,
            (lambda entry: entry >= 0) if last and before is None else wanted,
            picked, tiles_ref, ring, sems, tile_bits, prepare, multiply, add,
        )
        if last:
            for s in range(sources):
                keep[:, s * BLK : (s + 1) * BLK] = total[s, :cols, :]
                send[:, s * BLK : (s + 1) * BLK] = total[s, cols:, :].astype(BF16)

    slots = tiles.shape[0]
    sums = (sources, columns, BLK)
    if last:
        outs = [
            jax.ShapeDtypeStruct((cols, sources * BLK), F32),
            jax.ShapeDtypeStruct((cols, sources * BLK), BF16),
        ]
    else:
        outs = [jax.ShapeDtypeStruct(sums, F32)]
    return call(
        body,
        "spread_back",
        outs,
        [SMEM_SPEC, HBM_SPEC] + [VMEM_SPEC] * (len(given) + len(extra)),
        [pltpu.VMEM((spare + 1, columns, BLK), BF16)]
        + ([pltpu.VMEM(sums, F32)] if last else [])
        + ring_scratch(tiles.shape[0]),
        slots * BLK * BLK * columns,
        slots * BLK * BLK,
    )(meta, tiles, *given, *extra)


def spot_order(chips):
    at = lax.axis_index("wide")
    chip, core = at >> 1, at & 1
    return [
        2 * lax.rem(chip + s, chips) + (core if k == 0 else 1 - core) for s in range(chips) for k in range(2)
    ]


def layer(near, far, weight, bias, cotangent, cols, chips):
    rows, hidden = cotangent.shape
    near_cols = near[0].shape[1]
    step = 2 * BLK if rows % (2 * BLK) == 0 else BLK

    def body(*refs):
        near_refs = refs[: len(near)]
        far_refs = refs[len(near) : len(near) + len(far)]
        weight_ref, bias_ref, cot_ref = refs[len(near) + len(far) : len(near) + len(far) + 3]
        act_ref, near_out, far_out, near_mix, far_mix, delta_ref, ordered = refs[
            len(near) + len(far) + 3 :
        ]
        for part, owner in enumerate(spot_order(chips)):
            low = pl.multiple_of(owner * cols, cols)
            ordered[part * cols : (part + 1) * cols, :] = weight_ref[pl.ds(low, cols), :]
        for low in range(0, rows, step):
            now = slice(low, low + step)
            mixed = []
            for group, out in ((near_refs, near_mix), (far_refs, far_mix)):
                value = group[0][now, :].astype(F32)
                for ref in group[1:]:
                    value = value + ref[now, :].astype(F32)
                mixed.append(value.astype(BF16))
                out[now, :] = mixed[-1]
            pre = jnp.dot(mixed[0], ordered[:near_cols, :], preferred_element_type=F32)
            pre = pre + jnp.dot(mixed[1], ordered[near_cols:, :], preferred_element_type=F32)
            pre = pre + bias_ref[...].astype(F32)
            square = pre * pre
            bend = jnp.tanh(ROOT * pre * (1.0 + CUBIC * square))
            half = 0.5 * (1.0 + bend)
            act_ref[now, :] = (pre * half).astype(BF16)
            slope = half + 0.5 * ROOT * pre * (1.0 - bend * bend) * (1.0 + 3.0 * CUBIC * square)
            delta = (cot_ref[now, :].astype(F32) * slope).astype(BF16)
            delta_ref[now, :] = delta
            turned = lax.dot_general(
                ordered[...], delta, (((1,), (1,)), ((), ())), preferred_element_type=F32
            ).astype(BF16)
            near_out[:, now] = turned[:near_cols, :]
            far_out[:, now] = turned[near_cols:, :]

    return call(
        body,
        "layer",
        [
            jax.ShapeDtypeStruct((rows, hidden), BF16),
            jax.ShapeDtypeStruct((near_cols, rows), BF16),
            jax.ShapeDtypeStruct((hidden - near_cols, rows), BF16),
            jax.ShapeDtypeStruct((rows, near_cols), BF16),
            jax.ShapeDtypeStruct((rows, hidden - near_cols), BF16),
            jax.ShapeDtypeStruct((rows, hidden), BF16),
        ],
        [VMEM_SPEC] * (len(near) + len(far) + 3),
        [pltpu.VMEM((hidden, hidden), BF16)],
        4 * rows * hidden * hidden,
        10 * rows * hidden,
    )(*near, *far, weight, bias, cotangent)


def weight_parts(near_mix, far_mix, delta, cols, chips):
    rows, near_cols = near_mix.shape
    hidden = delta.shape[1]
    lines = cols + 8

    def body(near_ref, far_ref, delta_ref, grad_ref):
        tail = jnp.broadcast_to(
            jnp.sum(delta_ref[...].astype(F32), axis=0, keepdims=True), (8, hidden)
        )
        grads = [
            lax.dot_general(
                ref[...], delta_ref[...], (((0,), (0,)), ((), ())), preferred_element_type=F32
            )
            for ref in (near_ref, far_ref)
        ]
        for part in range(2 * chips):
            source = grads[0] if part < 2 else grads[1]
            low = part * cols - (0 if part < 2 else near_cols)
            grad_ref[part % 2, part // 2, :cols, :] = source[low : low + cols, :]
            grad_ref[part % 2, part // 2, cols:, :] = tail

    return call(
        body,
        "weight_parts",
        [jax.ShapeDtypeStruct((2, chips, lines, hidden), F32)],
        [VMEM_SPEC] * 3,
        [],
        2 * rows * hidden * hidden,
        6 * rows * hidden,
    )(near_mix, far_mix, delta)[0]


def weight_sums(way, pieces, top, lines, packed, hidden):
    n_rows = lax.axis_size("rows")
    width = pieces[0].shape[1] // hidden

    def body(*refs):
        out, held = refs[-2:]
        for i in range(n_rows):
            ref = refs[i // (n_rows // len(pieces))]
            low = (i % (n_rows // len(pieces))) * (ref.shape[0] // (n_rows // len(pieces))) + top
            place = row_at(way, i)
            for k in range(width):
                rows = min(packed, lines - k * packed)
                if rows > 0:
                    part = ref[low : low + packed, k * hidden : (k + 1) * hidden].astype(F32)
                    held[place, k * packed : k * packed + rows, :] = part[:rows]
        value = held[0]
        for r in range(1, n_rows):
            value = value + held[r]
        out[...] = value

    return call(
        body,
        "weight_sums",
        [jax.ShapeDtypeStruct((lines, hidden), F32)],
        [VMEM_SPEC] * len(pieces),
        [pltpu.VMEM((n_rows, lines, hidden), F32)],
        0,
        8 * lines * hidden,
    )(*pieces)[0]


def assemble(mine, other, cols, chips):
    hidden = mine[0].shape[1]

    def body(*refs):
        out, bias_out = refs[-2:]
        for part, owner in enumerate(spot_order(chips)):
            low = pl.multiple_of(owner * cols, cols)
            out[pl.ds(low, cols), :] = refs[(part % 2) * chips + part // 2][:cols, :]
        bias_out[...] = refs[0][cols : cols + 1, :]

    return call(
        body,
        "assemble",
        [
            jax.ShapeDtypeStruct((2 * chips * cols, hidden), F32),
            jax.ShapeDtypeStruct((1, hidden), F32),
        ],
        [VMEM_SPEC] * (2 * chips),
        [],
        0,
        8 * chips * cols * hidden,
    )(*mine, *other)


def per_device(features, tile_weights, tile_source, tile_dest, tile_count, weight, bias, cotangent):
    cols, width = features.shape
    sources = width // BLK
    slots = tile_weights.shape[0]
    hidden = weight.shape[0]
    wide = lax.axis_size("wide")
    chips = wide // 2
    n_rows = lax.axis_size("rows")
    chunk = sources // wide
    near_cols = 2 * cols
    lines = cols + 8
    tile_bits, source_bits = bits_of(slots), bits_of(sources)

    at = lax.axis_index("wide")
    chip, core = at >> 1, at & 1

    def swap_cores(value):
        return lax.ppermute(value, "wide", [(i, i ^ 1) for i in range(wide)])

    def from_chip(value, shift):
        pairs = [(2 * ((i + shift) % chips) + k, 2 * i + k) for i in range(chips) for k in range(2)]
        return lax.ppermute(value, "wide", pairs)

    def along(value, pairs):
        return lax.ppermute(value, "rows", pairs)

    def around(value, shift):
        return along(value, [(i, (i + shift) % n_rows) for i in range(n_rows)])

    beside, across_pairs = [(0, 1), (1, 0), (2, 3), (3, 2)], [(0, 2), (1, 3), (2, 0), (3, 1)]

    def known(way):
        return way if n_rows == 4 or way == "all" else "direct"

    def gathered(way, value):
        if way == "all":
            return [lax.all_gather(value, "rows", axis=0, tiled=True)]
        if way == "direct":
            return [value] + [around(value, -s) for s in range(1, n_rows)]
        got_skip = along(value, across_pairs)
        got_next = along(value, beside)
        return [value, got_next, got_skip, along(got_skip, beside)]

    def tied(value, other):
        return lax.optimization_barrier((value, other))[0]

    parts = [features, swap_cores(features)]

    def split(value, size):
        whole = ((value.astype(F32) + 0.5) * (1.0 / size)).astype(jnp.int32)
        return whole, value - whole * size

    slot = jnp.arange(slots, dtype=jnp.int32)
    owner, within = split(tile_dest, sources)
    holder, nth = split(within, chunk)
    away = (holder >> 1) - chip
    away = jnp.where(away < 0, away + chips, away)
    per_row = chips * chunk
    nth_bits = bits_of(per_row)
    layout = (tile_bits, source_bits, nth_bits)
    place = (owner << nth_bits) | (away * chunk + nth)
    ours = (slot < tile_count[0]) & ((holder & 1) == core)
    meta = (place << (source_bits + tile_bits)) | (tile_source << tile_bits) | slot
    meta = jnp.where(ours, meta, -1)

    def partial_sums(owners, way, cuts):
        return aggregate(meta, tile_weights, parts, owners, way, cuts, layout)

    cuts = (0, chunk, per_row)
    if known("pair") == "pair":
        (relayed,) = partial_sums([3], "pair", (0, per_row))
        next_near, next_far, skip_near, skip_far = partial_sums([1, 2], "pair", cuts)
        own_near, own_far = partial_sums([0], "pair", cuts)
        passed = along(relayed, beside)
        if QTIE:
            next_near, next_far = tied((next_near, next_far), passed)
        edge = chunk * BLK

        def merged(value, other):
            return (value.astype(F32) + other.astype(F32)).astype(BF16)

        far_terms = [
            own_far,
            along(next_far, beside),
            along(merged(skip_far, passed[edge:]), across_pairs),
        ]
        near = [
            own_near,
            along(next_near, beside),
            along(merged(skip_near, passed[:edge]), across_pairs),
        ]
    else:
        outs = partial_sums(list(range(n_rows)), "direct", cuts)
        near = [outs[0]] + [around(outs[2 * s], s) for s in range(1, n_rows)]
        far_terms = [outs[1]] + [around(outs[2 * s + 1], s) for s in range(1, n_rows)]
    passing = far_terms[0]
    for term in far_terms[1:]:
        passing = passing + term.astype(F32)
    passing = passing.astype(BF16).reshape(chips - 1, chunk * BLK, near_cols)
    far = [from_chip(passing[chips - s - 1], s) for s in range(1, chips)]
    far = far[0] if chips == 2 else jnp.concatenate(far, axis=1)

    activation, near_prop, far_prop, near_mix, far_mix, delta = layer(
        near, [far], weight, bias.reshape(1, hidden), cotangent, cols, chips
    )

    near_all = gathered(known(AG_NEAR), near_prop)
    far_prop = far_prop.reshape(chips - 1, near_cols, chunk * BLK)
    across = (chips - 1) * chunk * BLK // hidden
    packed = -(-lines // across)
    spare = -(-packed // 16) * 16

    def pack(value):
        value = jnp.pad(value.astype(BF16), ((0, across * packed - lines), (0, 0)))
        value = jnp.concatenate([value[k * packed : (k + 1) * packed] for k in range(across)], axis=1)
        return jnp.pad(value, ((0, spare - packed), (0, 0)))

    grads = weight_parts(near_mix, far_mix, delta, cols, chips)
    part = grads[0] + swap_cores(grads[1])
    if XG and chips == 2:
        both = from_chip(jnp.concatenate([far_prop[0], pack(part[1])], axis=0), 1)
        extra = (both[near_cols:].astype(F32) + pack(part[0]).astype(F32)).astype(BF16)
        payload = jnp.concatenate([both[:near_cols], extra], axis=0)
    else:
        coming = [from_chip(far_prop[chips - s - 1], s) for s in range(1, chips)]
        coming = coming[0] if chips == 2 else jnp.concatenate(coming, axis=1)
        quarter = part[0]
        for s in range(1, chips):
            quarter = quarter + from_chip(part[chips - s], s)
        payload = jnp.concatenate([coming, pack(quarter)], axis=0)
    if TIE:
        payload = tied(payload, near_all[2:3] if TIE == 1 else near_all[1:3])
    far_way = known(AG_FAR)
    far_all = gathered(far_way, payload)

    def pieces_of(way, arrays, first, count, only=None):
        each = n_rows // len(arrays)
        found = []
        for i in range(n_rows) if only is None else only:
            array = arrays[i // each]
            found.append((array, (i % each) * (array.shape[0] // each), way, i, first, count))
        return found

    near_pieces = pieces_of(known(AG_NEAR), near_all, 0, chunk)
    common = (near_cols, sources, per_row, layout, cols)
    if SPLIT and far_way == "pair":
        early = near_pieces + pieces_of(far_way, far_all, chunk, per_row - chunk, (0, 1, 2))
        late = pieces_of(far_way, far_all, chunk, per_row - chunk, (3,))
        (before,) = spread_back(meta, tile_weights, early, None, *common, False)
        keep, send = spread_back(meta, tile_weights, late, before, *common, True)
    else:
        every = near_pieces + pieces_of(far_way, far_all, chunk, per_row - chunk)
        keep, send = spread_back(meta, tile_weights, every, None, *common, True)
    grad_features = (keep + swap_cores(send).astype(F32)).astype(BF16)

    quarter = weight_sums(known(AG_FAR), far_all, near_cols, lines, packed, hidden)
    half = [quarter] + [from_chip(quarter, s) for s in range(1, chips)]
    other_half = swap_cores(jnp.stack(half))
    grad_weight, grad_bias = assemble(half, [other_half[s] for s in range(chips)], cols, chips)
    return (activation, grad_features, grad_weight, grad_bias.reshape(hidden))


def solution(mesh):
    in_specs = (
        P("wide", ("groups", "rows")),
        P(("groups", "rows"), None, None),
        P(("groups", "rows")),
        P(("groups", "rows")),
        P(("groups", "rows")),
        P(),
        P(),
        P(("groups", "rows", "wide"), None),
    )
    out_specs = (
        P(("groups", "rows", "wide"), None),
        P("wide", ("groups", "rows")),
        P("groups", None),
        P("groups"),
    )
    return jax.shard_map(
        per_device, mesh=mesh, in_specs=in_specs, out_specs=out_specs, check_vma=False
    )
```

```python
import functools
import math

import jax
import jax.numpy as jnp
from jax import lax
from jax.experimental import pallas as pl
from jax.experimental.pallas import tpu as pltpu
from jax.sharding import PartitionSpec as P

BLK = 128
GROUP = 16
GROUP_BACK = 16
ROWS_UNIT = 8
LATE = False
AG_NEAR = "pair"
AG_FAR = 'all'
TIE = 0
QTIE = 0
COST = 1
XG = False
SPLIT = False
RING = 4
VMEM_BYTES = 48 * 1024 * 1024
ROOT = math.sqrt(2.0 / math.pi)
CUBIC = 0.044715
BF16 = jnp.bfloat16
F32 = jnp.float32

SMEM_SPEC = pl.BlockSpec(memory_space=pltpu.SMEM)
VMEM_SPEC = pl.BlockSpec(memory_space=pltpu.VMEM)
HBM_SPEC = pl.BlockSpec(memory_space=pltpu.HBM)


def bits_of(size):
    return max(1, int(size).bit_length())


def call(body, name, out_shape, in_specs, scratch, flops, nbytes):
    return pl.pallas_call(
        body,
        name=name,
        out_shape=out_shape,
        in_specs=in_specs,
        out_specs=jax.tree.map(lambda _: VMEM_SPEC, out_shape),
        scratch_shapes=scratch,
        compiler_params=pltpu.CompilerParams(vmem_limit_bytes=VMEM_BYTES),
        cost_estimate=pl.CostEstimate(flops=COST * flops, bytes_accessed=COST * nbytes, transcendentals=0),
    )


def each_tile(
    meta, wanted, picked, tiles, ring, sems, tile_bits, prepare, multiply, add, size=GROUP
):
    total = meta.shape[0]
    depth = ring.shape[0] // size
    tile_mask = (1 << tile_bits) - 1

    def scan(step, found):
        for u in range(GROUP):
            entry = meta[step * GROUP + u]
            picked[found] = entry
            found = found + jnp.where(wanted(entry), 1, 0)
        return found

    found = lax.fori_loop(0, total // GROUP, scan, jnp.int32(0))
    for u in range(size):
        picked[found + u] = jnp.int32(-1)
    groups = lax.div(found + (size - 1), size)

    def copies(group):
        base = lax.rem(group, depth) * size
        for u in range(size):
            tile = jnp.maximum(picked[group * size + u], 0) & tile_mask
            yield pltpu.make_async_copy(tiles.at[tile], ring.at[base + u], sems.at[base + u])

    def start(group, carry):
        for copy in copies(group):
            copy.start()
        return carry

    lax.fori_loop(0, jnp.minimum(groups, depth), start, 0)
    prepare()

    def work(group, carry):
        for copy in copies(group):
            copy.wait()
        base = lax.rem(group, depth) * size
        entries = [picked[group * size + u] for u in range(size)]
        products = [multiply(entries[u], ring.at[base + u]) for u in range(size)]
        for u in range(size):
            add(entries[u], products[u])

        @pl.when(group + depth < groups)
        def _():
            start(group + depth, 0)

        return carry

    lax.fori_loop(0, groups, work, 0)


def ring_scratch(slots):
    return [
        pltpu.SMEM((slots + 2 * GROUP,), jnp.int32),
        pltpu.VMEM((RING * GROUP, BLK, BLK), BF16),
        pltpu.SemaphoreType.DMA((RING * GROUP,)),
    ]


def row_at(way, i):
    count = lax.axis_size("rows")
    row = lax.axis_index("rows")
    if way == "all":
        return i
    if way == "direct":
        return lax.rem(row + (i % count), count)
    return row ^ i


def aggregate(meta, tiles, parts, owners, way, cuts, layout):
    tile_bits, source_bits, nth_bits = layout
    columns = sum(part.shape[0] for part in parts)
    sources = parts[0].shape[1] // BLK
    n_rows, per_row = lax.axis_size("rows"), cuts[-1]
    dead = n_rows * per_row
    pieces = list(zip(cuts[:-1], cuts[1:]))
    shapes = [
        jax.ShapeDtypeStruct(((high - low) * BLK, columns), F32 if i == 0 else BF16)
        for i in owners
        for low, high in pieces
    ]
    many = len(owners) == n_rows

    def body(meta_ref, tiles_ref, own_ref, *refs):
        part_refs = refs[: len(parts) - 1]
        outs = refs[len(parts) - 1 : len(parts) - 1 + len(shapes)]
        own, own_sem, turned, total, picked, ring, sems = refs[len(parts) - 1 + len(shapes) :]
        fetch = pltpu.make_async_copy(own_ref, own, own_sem)
        fetch.start()
        rows = [row_at(way, i) for i in owners]

        def prepare():
            fetch.wait()
            if many:
                total[...] = jnp.zeros_like(total)
            else:
                total[dead] = jnp.zeros_like(total[dead])
                for row in rows:
                    total[pl.ds(row * per_row, per_row)] = jnp.zeros((per_row, BLK, columns), F32)
            for s in range(sources):
                now = slice(s * BLK, (s + 1) * BLK)
                block = jnp.concatenate([own[:, now]] + [ref[:, now] for ref in part_refs], axis=0)
                turned[s] = jnp.transpose(block)

        def multiply(entry, tile):
            source = (jnp.maximum(entry, 0) >> tile_bits) & ((1 << source_bits) - 1)
            return jnp.dot(tile[...], turned[source], preferred_element_type=F32)

        def add(entry, product):
            rest = entry >> (tile_bits + source_bits)
            dest = (rest >> nth_bits) * per_row + (rest & ((1 << nth_bits) - 1))
            total[jnp.where(entry < 0, dead, dest)] += product

        def wanted(entry):
            if many:
                return entry >= 0
            owner = entry >> (tile_bits + source_bits + nth_bits)
            found = owner == rows[0]
            for row in rows[1:]:
                found = found | (owner == row)
            return found

        each_tile(
            meta_ref, wanted, picked, tiles_ref, ring, sems, tile_bits, prepare, multiply, add
        )
        spots = [(row * per_row + low, high - low) for row in rows for low, high in pieces]
        for out, (low, count) in zip(outs, spots):
            out[...] = total[pl.ds(low, count)].reshape(out.shape).astype(out.dtype)

    slots = tiles.shape[0]
    return call(
        body,
        "aggregate",
        shapes,
        [SMEM_SPEC, HBM_SPEC, HBM_SPEC] + [VMEM_SPEC] * (len(parts) - 1),
        [
            pltpu.VMEM(parts[0].shape, BF16),
            pltpu.SemaphoreType.DMA,
            pltpu.VMEM((sources, BLK, columns), BF16),
            pltpu.VMEM((dead + 1, BLK, columns), F32),
        ]
        + ring_scratch(tiles.shape[0]),
        slots * BLK * BLK * columns,
        slots * BLK * BLK,
    )(meta, tiles, *parts)


def spread_back(meta, tiles, pieces, before, columns, sources, per_row, layout, cols, last):
    tile_bits, source_bits, nth_bits = layout
    given = []
    for piece in pieces:
        if not any(piece[0] is other for other in given):
            given.append(piece[0])
    extra = [] if before is None else [before]
    spare = lax.axis_size("rows") * per_row

    def body(meta_ref, tiles_ref, *refs):
        rest = refs[len(given) + len(extra) :]
        if last:
            keep, send, held, total, picked, ring, sems = rest
        else:
            total, held, picked, ring, sems = rest
        rows = [row_at(way, i) for _, _, way, i, _, _ in pieces]

        def prepare():
            if before is None:
                total[...] = jnp.zeros_like(total)
            else:
                total[...] = refs[len(given)][...]
            held[spare] = jnp.zeros_like(held[spare])
            for (array, line, _, _, first, count), row in zip(pieces, rows):
                ref = next(ref for ref, other in zip(refs, given) if other is array)
                for q in range(count):
                    held[row * per_row + first + q] = ref[
                        line : line + columns, q * BLK : (q + 1) * BLK
                    ]

        def wanted(entry):
            rest = entry >> (tile_bits + source_bits)
            owner, nth = rest >> nth_bits, rest & ((1 << nth_bits) - 1)
            found = owner < 0
            for (_, _, _, _, first, count), row in zip(pieces, rows):
                found = found | ((owner == row) & (nth >= first) & (nth < first + count))
            return found & (entry >= 0)

        def multiply(entry, tile):
            rest = entry >> (tile_bits + source_bits)
            dest = (rest >> nth_bits) * per_row + (rest & ((1 << nth_bits) - 1))
            dest = jnp.where(entry < 0, spare, dest)
            return jnp.dot(held[dest], tile[...], preferred_element_type=F32)

        def add(entry, product):
            source = (jnp.maximum(entry, 0) >> tile_bits) & ((1 << source_bits) - 1)
            total[source] += product

        each_tile(
            meta_ref,
            (lambda entry: entry >= 0) if last and before is None else wanted,
            picked, tiles_ref, ring, sems, tile_bits, prepare, multiply, add,
            GROUP_BACK,
        )
        if last:
            for s in range(sources):
                keep[:, s * BLK : (s + 1) * BLK] = total[s, :cols, :]
                send[:, s * BLK : (s + 1) * BLK] = total[s, cols:, :].astype(BF16)

    slots = tiles.shape[0]
    sums = (sources, columns, BLK)
    if last:
        outs = [
            jax.ShapeDtypeStruct((cols, sources * BLK), F32),
            jax.ShapeDtypeStruct((cols, sources * BLK), BF16),
        ]
    else:
        outs = [jax.ShapeDtypeStruct(sums, F32)]
    return call(
        body,
        "spread_back",
        outs,
        [SMEM_SPEC, HBM_SPEC] + [VMEM_SPEC] * (len(given) + len(extra)),
        [pltpu.VMEM((spare + 1, columns, BLK), BF16)]
        + ([pltpu.VMEM(sums, F32)] if last else [])
        + ring_scratch(tiles.shape[0]),
        slots * BLK * BLK * columns,
        slots * BLK * BLK,
    )(meta, tiles, *given, *extra)


def spot_order(chips):
    at = lax.axis_index("wide")
    chip, core = at >> 1, at & 1
    return [
        2 * lax.rem(chip + s, chips) + (core if k == 0 else 1 - core) for s in range(chips) for k in range(2)
    ]


def layer(near, far, weight, bias, cotangent, cols, chips):
    rows, hidden = cotangent.shape
    near_cols = near[0].shape[1]
    step = 2 * BLK if rows % (2 * BLK) == 0 else BLK

    def body(*refs):
        near_refs = refs[: len(near)]
        far_refs = refs[len(near) : len(near) + len(far)]
        weight_ref, bias_ref, cot_ref = refs[len(near) + len(far) : len(near) + len(far) + 3]
        act_ref, near_out, far_out, near_mix, far_mix, delta_ref, ordered = refs[
            len(near) + len(far) + 3 :
        ]
        for part, owner in enumerate(spot_order(chips)):
            low = pl.multiple_of(owner * cols, cols)
            ordered[part * cols : (part + 1) * cols, :] = weight_ref[pl.ds(low, cols), :]
        for low in range(0, rows, step):
            now = slice(low, low + step)
            mixed = []
            for group, out in ((near_refs, near_mix), (far_refs, far_mix)):
                value = group[0][now, :].astype(F32)
                for ref in group[1:]:
                    value = value + ref[now, :].astype(F32)
                mixed.append(value.astype(BF16))
                out[now, :] = mixed[-1]
            pre = jnp.dot(mixed[0], ordered[:near_cols, :], preferred_element_type=F32)
            pre = pre + jnp.dot(mixed[1], ordered[near_cols:, :], preferred_element_type=F32)
            pre = pre + bias_ref[...].astype(F32)
            square = pre * pre
            bend = jnp.tanh(ROOT * pre * (1.0 + CUBIC * square))
            half = 0.5 * (1.0 + bend)
            act_ref[now, :] = (pre * half).astype(BF16)
            slope = half + 0.5 * ROOT * pre * (1.0 - bend * bend) * (1.0 + 3.0 * CUBIC * square)
            delta = (cot_ref[now, :].astype(F32) * slope).astype(BF16)
            delta_ref[now, :] = delta
            turned = lax.dot_general(
                ordered[...], delta, (((1,), (1,)), ((), ())), preferred_element_type=F32
            ).astype(BF16)
            near_out[:, now] = turned[:near_cols, :]
            far_out[:, now] = turned[near_cols:, :]

    return call(
        body,
        "layer",
        [
            jax.ShapeDtypeStruct((rows, hidden), BF16),
            jax.ShapeDtypeStruct((near_cols, rows), BF16),
            jax.ShapeDtypeStruct((hidden - near_cols, rows), BF16),
            jax.ShapeDtypeStruct((rows, near_cols), BF16),
            jax.ShapeDtypeStruct((rows, hidden - near_cols), BF16),
            jax.ShapeDtypeStruct((rows, hidden), BF16),
        ],
        [VMEM_SPEC] * (len(near) + len(far) + 3),
        [pltpu.VMEM((hidden, hidden), BF16)],
        4 * rows * hidden * hidden,
        10 * rows * hidden,
    )(*near, *far, weight, bias, cotangent)


def weight_parts(near_mix, far_mix, delta, cols, chips):
    rows, near_cols = near_mix.shape
    hidden = delta.shape[1]
    lines = cols + 8

    def body(near_ref, far_ref, delta_ref, grad_ref):
        tail = jnp.broadcast_to(
            jnp.sum(delta_ref[...].astype(F32), axis=0, keepdims=True), (8, hidden)
        )
        grads = [
            lax.dot_general(
                ref[...], delta_ref[...], (((0,), (0,)), ((), ())), preferred_element_type=F32
            )
            for ref in (near_ref, far_ref)
        ]
        for part in range(2 * chips):
            source = grads[0] if part < 2 else grads[1]
            low = part * cols - (0 if part < 2 else near_cols)
            grad_ref[part % 2, part // 2, :cols, :] = source[low : low + cols, :]
            grad_ref[part % 2, part // 2, cols:, :] = tail

    return call(
        body,
        "weight_parts",
        [jax.ShapeDtypeStruct((2, chips, lines, hidden), F32)],
        [VMEM_SPEC] * 3,
        [],
        2 * rows * hidden * hidden,
        6 * rows * hidden,
    )(near_mix, far_mix, delta)[0]


def weight_sums(way, pieces, top, lines, packed, hidden):
    n_rows = lax.axis_size("rows")
    width = pieces[0].shape[1] // hidden

    def body(*refs):
        out, held = refs[-2:]
        for i in range(n_rows):
            ref = refs[i // (n_rows // len(pieces))]
            low = (i % (n_rows // len(pieces))) * (ref.shape[0] // (n_rows // len(pieces))) + top
            place = row_at(way, i)
            for k in range(width):
                rows = min(packed, lines - k * packed)
                if rows > 0:
                    part = ref[low : low + packed, k * hidden : (k + 1) * hidden].astype(F32)
                    held[place, k * packed : k * packed + rows, :] = part[:rows]
        value = held[0]
        for r in range(1, n_rows):
            value = value + held[r]
        out[...] = value

    return call(
        body,
        "weight_sums",
        [jax.ShapeDtypeStruct((lines, hidden), F32)],
        [VMEM_SPEC] * len(pieces),
        [pltpu.VMEM((n_rows, lines, hidden), F32)],
        0,
        8 * lines * hidden,
    )(*pieces)[0]


def assemble(keep, got, mine, other, cols, chips):
    hidden = mine[0].shape[1]

    def body(keep_ref, got_ref, *refs):
        grad_ref, out, bias_out = refs[-3:]
        grad_ref[...] = (keep_ref[...] + got_ref[...].astype(F32)).astype(BF16)
        for part, owner in enumerate(spot_order(chips)):
            low = pl.multiple_of(owner * cols, cols)
            out[pl.ds(low, cols), :] = refs[(part % 2) * chips + part // 2][:cols, :]
        bias_out[...] = refs[0][cols : cols + 1, :]

    return call(
        body,
        "assemble",
        [
            jax.ShapeDtypeStruct(keep.shape, BF16),
            jax.ShapeDtypeStruct((2 * chips * cols, hidden), F32),
            jax.ShapeDtypeStruct((1, hidden), F32),
        ],
        [VMEM_SPEC] * (2 + 2 * chips),
        [],
        0,
        8 * chips * cols * hidden,
    )(keep, got, *mine, *other)


def per_device(features, tile_weights, tile_source, tile_dest, tile_count, weight, bias, cotangent):
    cols, width = features.shape
    sources = width // BLK
    slots = tile_weights.shape[0]
    hidden = weight.shape[0]
    wide = lax.axis_size("wide")
    chips = wide // 2
    n_rows = lax.axis_size("rows")
    chunk = sources // wide
    near_cols = 2 * cols
    lines = cols + 8
    tile_bits, source_bits = bits_of(slots), bits_of(sources)

    at = lax.axis_index("wide")
    chip, core = at >> 1, at & 1

    def swap_cores(value):
        return lax.ppermute(value, "wide", [(i, i ^ 1) for i in range(wide)])

    def from_chip(value, shift):
        pairs = [(2 * ((i + shift) % chips) + k, 2 * i + k) for i in range(chips) for k in range(2)]
        return lax.ppermute(value, "wide", pairs)

    def along(value, pairs):
        return lax.ppermute(value, "rows", pairs)

    def around(value, shift):
        return along(value, [(i, (i + shift) % n_rows) for i in range(n_rows)])

    beside, across_pairs = [(0, 1), (1, 0), (2, 3), (3, 2)], [(0, 2), (1, 3), (2, 0), (3, 1)]

    def known(way):
        return way if n_rows == 4 or way == "all" else "direct"

    def gathered(way, value):
        if way == "all":
            return [lax.all_gather(value, "rows", axis=0, tiled=True)]
        if way == "direct":
            return [value] + [around(value, -s) for s in range(1, n_rows)]
        got_skip = along(value, across_pairs)
        got_next = along(value, beside)
        return [value, got_next, got_skip, along(got_skip, beside)] if not LATE else [
            value, got_next, got_skip
        ]

    def tied(value, other):
        return lax.optimization_barrier((value, other))[0]

    parts = [features, swap_cores(features)]

    def split(value, size):
        whole = ((value.astype(F32) + 0.5) * (1.0 / size)).astype(jnp.int32)
        return whole, value - whole * size

    slot = jnp.arange(slots, dtype=jnp.int32)
    owner, within = split(tile_dest, sources)
    holder, nth = split(within, chunk)
    away = (holder >> 1) - chip
    away = jnp.where(away < 0, away + chips, away)
    per_row = chips * chunk
    nth_bits = bits_of(per_row)
    layout = (tile_bits, source_bits, nth_bits)
    place = (owner << nth_bits) | (away * chunk + nth)
    ours = (slot < tile_count[0]) & ((holder & 1) == core)
    meta = (place << (source_bits + tile_bits)) | (tile_source << tile_bits) | slot
    meta = jnp.where(ours, meta, -1)

    def partial_sums(owners, way, cuts):
        return aggregate(meta, tile_weights, parts, owners, way, cuts, layout)

    cuts = (0, chunk, per_row)
    if known("pair") == "pair":
        (relayed,) = partial_sums([3], "pair", (0, per_row))
        next_near, next_far, skip_near, skip_far = partial_sums([1, 2], "pair", cuts)
        own_near, own_far = partial_sums([0], "pair", cuts)
        passed = along(relayed, beside)
        if QTIE:
            next_near, next_far = tied((next_near, next_far), passed)
        edge = chunk * BLK

        def merged(value, other):
            return (value.astype(F32) + other.astype(F32)).astype(BF16)

        far_terms = [
            own_far,
            along(next_far, beside),
            along(merged(skip_far, passed[edge:]), across_pairs),
        ]
        near = [
            own_near,
            along(next_near, beside),
            along(merged(skip_near, passed[:edge]), across_pairs),
        ]
    else:
        outs = partial_sums(list(range(n_rows)), "direct", cuts)
        near = [outs[0]] + [around(outs[2 * s], s) for s in range(1, n_rows)]
        far_terms = [outs[1]] + [around(outs[2 * s + 1], s) for s in range(1, n_rows)]
    passing = far_terms[0]
    for term in far_terms[1:]:
        passing = passing + term.astype(F32)
    passing = passing.astype(BF16).reshape(chips - 1, chunk * BLK, near_cols)
    far = [from_chip(passing[chips - s - 1], s) for s in range(1, chips)]
    far = far[0] if chips == 2 else jnp.concatenate(far, axis=1)

    activation, near_prop, far_prop, near_mix, far_mix, delta = layer(
        near, [far], weight, bias.reshape(1, hidden), cotangent, cols, chips
    )

    near_all = gathered(known(AG_NEAR), near_prop)
    far_prop = far_prop.reshape(chips - 1, near_cols, chunk * BLK)
    across = (chips - 1) * chunk * BLK // hidden
    packed = -(-lines // across)
    spare = -(-packed // ROWS_UNIT) * ROWS_UNIT

    def pack(value):
        value = jnp.pad(value.astype(BF16), ((0, across * packed - lines), (0, 0)))
        value = jnp.concatenate([value[k * packed : (k + 1) * packed] for k in range(across)], axis=1)
        return jnp.pad(value, ((0, spare - packed), (0, 0)))

    grads = weight_parts(near_mix, far_mix, delta, cols, chips)
    part = grads[0] + swap_cores(grads[1])
    if XG and chips == 2:
        both = from_chip(jnp.concatenate([far_prop[0], pack(part[1])], axis=0), 1)
        extra = (both[near_cols:].astype(F32) + pack(part[0]).astype(F32)).astype(BF16)
        payload = jnp.concatenate([both[:near_cols], extra], axis=0)
    else:
        coming = [from_chip(far_prop[chips - s - 1], s) for s in range(1, chips)]
        coming = coming[0] if chips == 2 else jnp.concatenate(coming, axis=1)
        quarter = part[0]
        for s in range(1, chips):
            quarter = quarter + from_chip(part[chips - s], s)
        payload = jnp.concatenate([coming, pack(quarter)], axis=0)
    if TIE:
        payload = tied(payload, near_all[2:3] if TIE == 1 else near_all[1:3])
    far_way = known(AG_FAR)
    far_all = gathered(far_way, payload)
    if LATE and known(AG_NEAR) == "pair":
        near_all.append(along(tied(near_all[2], far_all[0]), beside))

    def pieces_of(way, arrays, first, count, only=None):
        each = n_rows // len(arrays)
        found = []
        for i in range(n_rows) if only is None else only:
            array = arrays[i // each]
            found.append((array, (i % each) * (array.shape[0] // each), way, i, first, count))
        return found

    near_pieces = pieces_of(known(AG_NEAR), near_all, 0, chunk)
    common = (near_cols, sources, per_row, layout, cols)
    if SPLIT and far_way == "pair":
        early = near_pieces + pieces_of(far_way, far_all, chunk, per_row - chunk, (0, 1, 2))
        late = pieces_of(far_way, far_all, chunk, per_row - chunk, (3,))
        (before,) = spread_back(meta, tile_weights, early, None, *common, False)
        keep, send = spread_back(meta, tile_weights, late, before, *common, True)
    else:
        every = near_pieces + pieces_of(far_way, far_all, chunk, per_row - chunk)
        keep, send = spread_back(meta, tile_weights, every, None, *common, True)
    got = swap_cores(send)
    quarter = weight_sums(known(AG_FAR), far_all, near_cols, lines, packed, hidden)
    half = [quarter] + [from_chip(quarter, s) for s in range(1, chips)]
    other_half = swap_cores(jnp.stack(half))
    grad_features, grad_weight, grad_bias = assemble(
        keep, got, half, [other_half[s] for s in range(chips)], cols, chips
    )
    return (activation, grad_features, grad_weight, grad_bias.reshape(hidden))


def solution(mesh):
    in_specs = (
        P("wide", ("groups", "rows")),
        P(("groups", "rows"), None, None),
        P(("groups", "rows")),
        P(("groups", "rows")),
        P(("groups", "rows")),
        P(),
        P(),
        P(("groups", "rows", "wide"), None),
    )
    out_specs = (
        P(("groups", "rows", "wide"), None),
        P("wide", ("groups", "rows")),
        P("groups", None),
        P("groups"),
    )
    return jax.shard_map(
        per_device, mesh=mesh, in_specs=in_specs, out_specs=out_specs, check_vma=False
    )
```

```python
import math

import jax
import jax.numpy as jnp
from jax import lax
from jax.experimental import pallas as pl
from jax.experimental.pallas import tpu as pltpu
from jax.sharding import PartitionSpec as P

BLK = 128
GROUP = 16
RING = 4
VMEM_BYTES = 48 * 1024 * 1024
ROOT = math.sqrt(2.0 / math.pi)
CUBIC = 0.044715
BF16 = jnp.bfloat16
F32 = jnp.float32

SMEM_SPEC = pl.BlockSpec(memory_space=pltpu.SMEM)
VMEM_SPEC = pl.BlockSpec(memory_space=pltpu.VMEM)
HBM_SPEC = pl.BlockSpec(memory_space=pltpu.HBM)


def bits_of(size):
    return max(1, int(size).bit_length())


def call(body, name, out_shape, in_specs, scratch, flops, nbytes):
    return pl.pallas_call(
        body,
        name=name,
        out_shape=out_shape,
        in_specs=in_specs,
        out_specs=jax.tree.map(lambda _: VMEM_SPEC, out_shape),
        scratch_shapes=scratch,
        compiler_params=pltpu.CompilerParams(vmem_limit_bytes=VMEM_BYTES),
        cost_estimate=pl.CostEstimate(flops=flops, bytes_accessed=nbytes, transcendentals=0),
    )


def each_tile(meta, wanted, picked, tiles, ring, sems, tile_bits, prepare, multiply, add):
    tile_mask = (1 << tile_bits) - 1

    def copies(group):
        base = lax.rem(group, RING) * GROUP
        for u in range(GROUP):
            tile = jnp.maximum(picked[group * GROUP + u], 0) & tile_mask
            yield pltpu.make_async_copy(tiles.at[tile], ring.at[base + u], sems.at[base + u])

    def start(group, carry):
        for copy in copies(group):
            copy.start()
        return carry

    def scan(step, state):
        found, begun = state
        for u in range(GROUP):
            entry = meta[step * GROUP + u]
            picked[found] = entry
            found = found + jnp.where(wanted(entry), 1, 0)
        full = (found >= (begun + 1) * GROUP) & (begun < RING)

        @pl.when(full)
        def _():
            start(begun, 0)

        return found, begun + jnp.where(full, 1, 0)

    zero = jnp.int32(0)
    found, begun = lax.fori_loop(0, meta.shape[0] // GROUP, scan, (zero, zero))
    for u in range(GROUP):
        picked[found + u] = jnp.int32(-1)
    groups = lax.div(found + (GROUP - 1), GROUP)
    lax.fori_loop(begun, jnp.minimum(groups, RING), start, 0)
    prepare()

    def work(group, carry):
        for copy in copies(group):
            copy.wait()
        base = lax.rem(group, RING) * GROUP
        entries = [picked[group * GROUP + u] for u in range(GROUP)]
        products = [multiply(entries[u], ring.at[base + u]) for u in range(GROUP)]
        for u in range(GROUP):
            add(entries[u], products[u])

        @pl.when(group + RING < groups)
        def _():
            start(group + RING, 0)

        return carry

    lax.fori_loop(0, groups, work, 0)


def ring_scratch(slots):
    return [
        pltpu.SMEM((slots + GROUP,), jnp.int32),
        pltpu.VMEM((RING * GROUP, BLK, BLK), BF16),
        pltpu.SemaphoreType.DMA((RING * GROUP,)),
    ]


def row_at(way, i):
    count = lax.axis_size("rows")
    row = lax.axis_index("rows")
    if way == "all":
        return i
    if way == "direct":
        return lax.rem(row + (i % count), count)
    return row ^ i


def aggregate(meta, tiles, parts, owners, way, cuts, layout):
    tile_bits, source_bits, nth_bits = layout
    columns = sum(part.shape[0] for part in parts)
    sources = parts[0].shape[1] // BLK
    n_rows, per_row = lax.axis_size("rows"), cuts[-1]
    dead = n_rows * per_row
    pieces = list(zip(cuts[:-1], cuts[1:]))
    shapes = [
        jax.ShapeDtypeStruct(((high - low) * BLK, columns), F32 if i == 0 else BF16)
        for i in owners
        for low, high in pieces
    ]
    many = len(owners) == n_rows

    def body(meta_ref, tiles_ref, own_ref, *refs):
        part_refs = refs[: len(parts) - 1]
        outs = refs[len(parts) - 1 : len(parts) - 1 + len(shapes)]
        own, own_sem, turned, total, picked, ring, sems = refs[len(parts) - 1 + len(shapes) :]
        fetch = pltpu.make_async_copy(own_ref, own, own_sem)
        fetch.start()
        rows = [row_at(way, i) for i in owners]

        def prepare():
            fetch.wait()
            if many:
                total[...] = jnp.zeros_like(total)
            else:
                total[dead] = jnp.zeros_like(total[dead])
                for row in rows:
                    total[pl.ds(row * per_row, per_row)] = jnp.zeros((per_row, BLK, columns), F32)
            for s in range(sources):
                now = slice(s * BLK, (s + 1) * BLK)
                block = jnp.concatenate([own[:, now]] + [ref[:, now] for ref in part_refs], axis=0)
                turned[s] = jnp.transpose(block)

        def multiply(entry, tile):
            source = (jnp.maximum(entry, 0) >> tile_bits) & ((1 << source_bits) - 1)
            return jnp.dot(tile[...], turned[source], preferred_element_type=F32)

        def add(entry, product):
            rest = entry >> (tile_bits + source_bits)
            dest = (rest >> nth_bits) * per_row + (rest & ((1 << nth_bits) - 1))
            total[jnp.where(entry < 0, dead, dest)] += product

        def wanted(entry):
            if many:
                return entry >= 0
            owner = entry >> (tile_bits + source_bits + nth_bits)
            found = owner == rows[0]
            for row in rows[1:]:
                found = found | (owner == row)
            return found

        each_tile(
            meta_ref, wanted, picked, tiles_ref, ring, sems, tile_bits, prepare, multiply, add
        )
        spots = [(row * per_row + low, high - low) for row in rows for low, high in pieces]
        for out, (low, count) in zip(outs, spots):
            out[...] = total[pl.ds(low, count)].reshape(out.shape).astype(out.dtype)

    slots = tiles.shape[0]
    return call(
        body,
        "aggregate",
        shapes,
        [SMEM_SPEC, HBM_SPEC, HBM_SPEC] + [VMEM_SPEC] * (len(parts) - 1),
        [
            pltpu.VMEM(parts[0].shape, BF16),
            pltpu.SemaphoreType.DMA,
            pltpu.VMEM((sources, BLK, columns), BF16),
            pltpu.VMEM((dead + 1, BLK, columns), F32),
        ]
        + ring_scratch(tiles.shape[0]),
        slots * BLK * BLK * columns,
        slots * BLK * BLK,
    )(meta, tiles, *parts)


def spread_back(meta, tiles, pieces, columns, sources, per_row, layout, cols):
    tile_bits, source_bits, nth_bits = layout
    given = []
    for piece in pieces:
        if not any(piece[0] is other for other in given):
            given.append(piece[0])
    spare = lax.axis_size("rows") * per_row

    def body(meta_ref, tiles_ref, *refs):
        keep, send, held, total, picked, ring, sems = refs[len(given) :]

        def prepare():
            total[...] = jnp.zeros_like(total)
            held[spare] = jnp.zeros_like(held[spare])
            for array, line, way, i, first, count in pieces:
                ref = next(ref for ref, other in zip(refs, given) if other is array)
                row = row_at(way, i)
                for q in range(count):
                    held[row * per_row + first + q] = ref[
                        line : line + columns, q * BLK : (q + 1) * BLK
                    ]

        def multiply(entry, tile):
            rest = entry >> (tile_bits + source_bits)
            dest = (rest >> nth_bits) * per_row + (rest & ((1 << nth_bits) - 1))
            dest = jnp.where(entry < 0, spare, dest)
            return jnp.dot(held[dest], tile[...], preferred_element_type=F32)

        def add(entry, product):
            source = (jnp.maximum(entry, 0) >> tile_bits) & ((1 << source_bits) - 1)
            total[source] += product

        each_tile(
            meta_ref, lambda entry: entry >= 0, picked, tiles_ref, ring, sems, tile_bits,
            prepare, multiply, add,
        )
        for s in range(sources):
            keep[:, s * BLK : (s + 1) * BLK] = total[s, :cols, :]
            send[:, s * BLK : (s + 1) * BLK] = total[s, cols:, :].astype(BF16)

    slots = tiles.shape[0]
    return call(
        body,
        "spread_back",
        [
            jax.ShapeDtypeStruct((cols, sources * BLK), F32),
            jax.ShapeDtypeStruct((cols, sources * BLK), BF16),
        ],
        [SMEM_SPEC, HBM_SPEC] + [VMEM_SPEC] * len(given),
        [
            pltpu.VMEM((spare + 1, columns, BLK), BF16),
            pltpu.VMEM((sources, columns, BLK), F32),
        ]
        + ring_scratch(tiles.shape[0]),
        slots * BLK * BLK * columns,
        slots * BLK * BLK,
    )(meta, tiles, *given)


def spot_order(chips):
    at = lax.axis_index("wide")
    chip, core = at >> 1, at & 1
    return [
        2 * lax.rem(chip + s, chips) + (core if k == 0 else 1 - core) for s in range(chips) for k in range(2)
    ]


def layer(near, far, weight, bias, cotangent, cols, chips):
    rows, hidden = cotangent.shape
    near_cols = near[0].shape[1]
    step = 2 * BLK if rows % (2 * BLK) == 0 else BLK

    def body(*refs):
        near_refs = refs[: len(near)]
        far_refs = refs[len(near) : len(near) + len(far)]
        weight_ref, bias_ref, cot_ref = refs[len(near) + len(far) : len(near) + len(far) + 3]
        act_ref, near_out, far_out, near_mix, far_mix, delta_ref, ordered = refs[
            len(near) + len(far) + 3 :
        ]
        for part, owner in enumerate(spot_order(chips)):
            low = pl.multiple_of(owner * cols, cols)
            ordered[part * cols : (part + 1) * cols, :] = weight_ref[pl.ds(low, cols), :]
        for low in range(0, rows, step):
            now = slice(low, low + step)
            mixed = []
            for group, out in ((near_refs, near_mix), (far_refs, far_mix)):
                value = group[0][now, :].astype(F32)
                for ref in group[1:]:
                    value = value + ref[now, :].astype(F32)
                mixed.append(value.astype(BF16))
                out[now, :] = mixed[-1]
            pre = jnp.dot(mixed[0], ordered[:near_cols, :], preferred_element_type=F32)
            pre = pre + jnp.dot(mixed[1], ordered[near_cols:, :], preferred_element_type=F32)
            pre = pre + bias_ref[...].astype(F32)
            square = pre * pre
            bend = jnp.tanh(ROOT * pre * (1.0 + CUBIC * square))
            half = 0.5 * (1.0 + bend)
            act_ref[now, :] = (pre * half).astype(BF16)
            slope = half + 0.5 * ROOT * pre * (1.0 - bend * bend) * (1.0 + 3.0 * CUBIC * square)
            delta = (cot_ref[now, :].astype(F32) * slope).astype(BF16)
            delta_ref[now, :] = delta
            turned = lax.dot_general(
                ordered[...], delta, (((1,), (1,)), ((), ())), preferred_element_type=F32
            ).astype(BF16)
            near_out[:, now] = turned[:near_cols, :]
            far_out[:, now] = turned[near_cols:, :]

    return call(
        body,
        "layer",
        [
            jax.ShapeDtypeStruct((rows, hidden), BF16),
            jax.ShapeDtypeStruct((near_cols, rows), BF16),
            jax.ShapeDtypeStruct((hidden - near_cols, rows), BF16),
            jax.ShapeDtypeStruct((rows, near_cols), BF16),
            jax.ShapeDtypeStruct((rows, hidden - near_cols), BF16),
            jax.ShapeDtypeStruct((rows, hidden), BF16),
        ],
        [VMEM_SPEC] * (len(near) + len(far) + 3),
        [pltpu.VMEM((hidden, hidden), BF16)],
        4 * rows * hidden * hidden,
        10 * rows * hidden,
    )(*near, *far, weight, bias, cotangent)


def weight_parts(near_mix, far_mix, delta, cols, chips):
    rows, near_cols = near_mix.shape
    hidden = delta.shape[1]
    lines = cols + 8

    def body(near_ref, far_ref, delta_ref, grad_ref):
        tail = jnp.broadcast_to(
            jnp.sum(delta_ref[...].astype(F32), axis=0, keepdims=True), (8, hidden)
        )
        grads = [
            lax.dot_general(
                ref[...], delta_ref[...], (((0,), (0,)), ((), ())), preferred_element_type=F32
            )
            for ref in (near_ref, far_ref)
        ]
        for part in range(2 * chips):
            source = grads[0] if part < 2 else grads[1]
            low = part * cols - (0 if part < 2 else near_cols)
            grad_ref[part % 2, part // 2, :cols, :] = source[low : low + cols, :]
            grad_ref[part % 2, part // 2, cols:, :] = tail

    return call(
        body,
        "weight_parts",
        [jax.ShapeDtypeStruct((2, chips, lines, hidden), F32)],
        [VMEM_SPEC] * 3,
        [],
        2 * rows * hidden * hidden,
        6 * rows * hidden,
    )(near_mix, far_mix, delta)[0]


def weight_sums(gathered, n_rows, top, lines, packed, hidden):
    tall, width = gathered.shape[0] // n_rows, gathered.shape[1] // hidden

    def body(ref, out):
        for k in range(width):
            rows = min(packed, lines - k * packed)
            if rows > 0:
                value = jnp.zeros((packed, hidden), F32)
                for row in range(n_rows):
                    low = row * tall + top
                    part = ref[low : low + packed, k * hidden : (k + 1) * hidden]
                    value = value + part.astype(F32)
                out[k * packed : k * packed + rows, :] = value[:rows]

    return call(
        body,
        "weight_sums",
        [jax.ShapeDtypeStruct((lines, hidden), F32)],
        [VMEM_SPEC],
        [],
        0,
        8 * lines * hidden,
    )(gathered)[0]


def assemble(keep, got, mine, other, cols, chips):
    hidden = mine[0].shape[1]

    def body(keep_ref, got_ref, *refs):
        grad_ref, out, bias_out = refs[-3:]
        grad_ref[...] = (keep_ref[...] + got_ref[...].astype(F32)).astype(BF16)
        for part, owner in enumerate(spot_order(chips)):
            low = pl.multiple_of(owner * cols, cols)
            out[pl.ds(low, cols), :] = refs[(part % 2) * chips + part // 2][:cols, :]
        bias_out[...] = refs[0][cols : cols + 1, :]

    return call(
        body,
        "assemble",
        [
            jax.ShapeDtypeStruct(keep.shape, BF16),
            jax.ShapeDtypeStruct((2 * chips * cols, hidden), F32),
            jax.ShapeDtypeStruct((1, hidden), F32),
        ],
        [VMEM_SPEC] * (2 + 2 * chips),
        [],
        0,
        8 * chips * cols * hidden,
    )(keep, got, *mine, *other)


def per_device(features, tile_weights, tile_source, tile_dest, tile_count, weight, bias, cotangent):
    cols, width = features.shape
    sources = width // BLK
    slots = tile_weights.shape[0]
    hidden = weight.shape[0]
    wide = lax.axis_size("wide")
    chips = wide // 2
    n_rows = lax.axis_size("rows")
    paired = n_rows == 4
    chunk = sources // wide
    per_row = chips * chunk
    near_cols = 2 * cols
    lines = cols + 8

    at = lax.axis_index("wide")
    chip, core = at >> 1, at & 1

    def swap_cores(value):
        return lax.ppermute(value, "wide", [(i, i ^ 1) for i in range(wide)])

    def from_chip(value, shift):
        pairs = [(2 * ((i + shift) % chips) + k, 2 * i + k) for i in range(chips) for k in range(2)]
        return lax.ppermute(value, "wide", pairs)

    def around(value, shift):
        return lax.ppermute(value, "rows", [(i, (i + shift) % n_rows) for i in range(n_rows)])

    def beside(value):
        return lax.ppermute(value, "rows", [(i, i ^ 1) for i in range(n_rows)])

    def across(value):
        return lax.ppermute(value, "rows", [(i, i ^ 2) for i in range(n_rows)])

    def tied(value, other):
        return lax.optimization_barrier((value, other))[0]

    parts = [features, swap_cores(features)]
    layout = tile_bits, source_bits, nth_bits = bits_of(slots), bits_of(sources), bits_of(per_row)

    def split(value, size):
        whole = ((value.astype(F32) + 0.5) * (1.0 / size)).astype(jnp.int32)
        return whole, value - whole * size

    slot = jnp.arange(slots, dtype=jnp.int32)
    owner, within = split(tile_dest, sources)
    holder, nth = split(within, chunk)
    away = (holder >> 1) - chip
    away = jnp.where(away < 0, away + chips, away)
    place = (owner << nth_bits) | (away * chunk + nth)
    ours = (slot < tile_count[0]) & ((holder & 1) == core)
    meta = (place << (source_bits + tile_bits)) | (tile_source << tile_bits) | slot
    meta = jnp.where(ours, meta, -1)

    def partial_sums(owners, way, cuts):
        return aggregate(meta, tile_weights, parts, owners, way, cuts, layout)

    cuts = (0, chunk, per_row)
    if paired:

        def merged(value, other):
            return (value.astype(F32) + other.astype(F32)).astype(BF16)

        (relayed,) = partial_sums([3], "pair", (0, per_row))
        near_1, far_1, near_2, far_2 = partial_sums([1, 2], "pair", cuts)
        near_0, far_0 = partial_sums([0], "pair", cuts)
        passed = beside(relayed)
        edge = chunk * BLK
        far_terms = [far_0, beside(far_1), across(merged(far_2, passed[edge:]))]
        near = [near_0, beside(near_1), across(merged(near_2, passed[:edge]))]
    else:
        outs = partial_sums(list(range(n_rows)), "direct", cuts)
        near = [outs[0]] + [around(outs[2 * s], s) for s in range(1, n_rows)]
        far_terms = [outs[1]] + [around(outs[2 * s + 1], s) for s in range(1, n_rows)]
    passing = far_terms[0]
    for term in far_terms[1:]:
        passing = passing + term.astype(F32)
    passing = passing.astype(BF16).reshape(chips - 1, chunk * BLK, near_cols)
    far = [from_chip(passing[chips - s - 1], s) for s in range(1, chips)]
    far = far[0] if chips == 2 else jnp.concatenate(far, axis=1)

    activation, near_prop, far_prop, near_mix, far_mix, delta = layer(
        near, [far], weight, bias.reshape(1, hidden), cotangent, cols, chips
    )

    far_prop = far_prop.reshape(chips - 1, near_cols, chunk * BLK)
    coming = [from_chip(far_prop[chips - s - 1], s) for s in range(1, chips)]
    coming = coming[0] if chips == 2 else jnp.concatenate(coming, axis=1)
    if paired:
        got_skip = across(near_prop)
        got_next = beside(near_prop)
        got_last = beside(tied(got_skip, coming))
        near_all = [near_prop, got_next, got_skip, got_last]
    else:
        near_all = [near_prop] + [around(near_prop, -s) for s in range(1, n_rows)]

    grads = weight_parts(near_mix, far_mix, delta, cols, chips)
    part = grads[0] + swap_cores(grads[1])
    quarter = part[0]
    for s in range(1, chips):
        quarter = quarter + from_chip(part[chips - s], s)
    width_in = coming.shape[1] // hidden
    packed = -(-lines // width_in)
    extra = jnp.pad(quarter.astype(BF16), ((0, width_in * packed - lines), (0, 0)))
    extra = jnp.concatenate([extra[k * packed : (k + 1) * packed] for k in range(width_in)], axis=1)
    extra = jnp.pad(extra, ((0, -packed % 8), (0, 0)))
    tall = near_cols + extra.shape[0]
    far_all = lax.all_gather(jnp.concatenate([coming, extra], axis=0), "rows", axis=0, tiled=True)

    way = "pair" if paired else "direct"
    pieces = [(array, 0, way, i, 0, chunk) for i, array in enumerate(near_all)]
    pieces += [(far_all, i * tall, "all", i, chunk, per_row - chunk) for i in range(n_rows)]
    keep, send = spread_back(
        meta, tile_weights, pieces, near_cols, sources, per_row, layout, cols
    )
    got = swap_cores(send)
    quarter = weight_sums(far_all, n_rows, near_cols, lines, packed, hidden)
    half = [quarter] + [from_chip(quarter, s) for s in range(1, chips)]
    other = swap_cores(jnp.stack(half))
    grad_features, grad_weight, grad_bias = assemble(
        keep, got, half, [other[s] for s in range(chips)], cols, chips
    )
    return (activation, grad_features, grad_weight, grad_bias.reshape(hidden))


def solution(mesh):
    in_specs = (
        P("wide", ("groups", "rows")),
        P(("groups", "rows"), None, None),
        P(("groups", "rows")),
        P(("groups", "rows")),
        P(("groups", "rows")),
        P(),
        P(),
        P(("groups", "rows", "wide"), None),
    )
    out_specs = (
        P(("groups", "rows", "wide"), None),
        P("wide", ("groups", "rows")),
        P("groups", None),
        P("groups"),
    )
    return jax.shard_map(
        per_device, mesh=mesh, in_specs=in_specs, out_specs=out_specs, check_vma=False
    )
```

```python
import math

import jax
import jax.numpy as jnp
from jax import lax
from jax.experimental import pallas as pl
from jax.experimental.pallas import tpu as pltpu
from jax.sharding import PartitionSpec as P

BLK = 128
GROUP = 16
RING = 4
VMEM_BYTES = 48 * 1024 * 1024
ROOT = math.sqrt(2.0 / math.pi)
CUBIC = 0.044715
BF16 = jnp.bfloat16
F32 = jnp.float32

SMEM_SPEC = pl.BlockSpec(memory_space=pltpu.SMEM)
VMEM_SPEC = pl.BlockSpec(memory_space=pltpu.VMEM)
HBM_SPEC = pl.BlockSpec(memory_space=pltpu.HBM)


def bits_of(size):
    return max(1, int(size).bit_length())


def call(body, name, out_shape, in_specs, scratch, flops, nbytes):
    return pl.pallas_call(
        body,
        name=name,
        out_shape=out_shape,
        in_specs=in_specs,
        out_specs=jax.tree.map(lambda _: VMEM_SPEC, out_shape),
        scratch_shapes=scratch,
        compiler_params=pltpu.CompilerParams(vmem_limit_bytes=VMEM_BYTES),
        cost_estimate=pl.CostEstimate(flops=flops, bytes_accessed=nbytes, transcendentals=0),
    )


def each_tile(meta, wanted, picked, tiles, ring, sems, tile_bits, prepare, multiply, add):
    tile_mask = (1 << tile_bits) - 1

    def copies(group):
        base = lax.rem(group, RING) * GROUP
        for u in range(GROUP):
            tile = jnp.maximum(picked[group * GROUP + u], 0) & tile_mask
            yield pltpu.make_async_copy(tiles.at[tile], ring.at[base + u], sems.at[base + u])

    def start(group, carry):
        for copy in copies(group):
            copy.start()
        return carry

    def scan(step, state):
        found, begun = state
        for u in range(GROUP):
            entry = meta[step * GROUP + u]
            picked[found] = entry
            found = found + jnp.where(wanted(entry), 1, 0)
        full = (found >= (begun + 1) * GROUP) & (begun < RING)

        @pl.when(full)
        def _():
            start(begun, 0)

        return found, begun + jnp.where(full, 1, 0)

    zero = jnp.int32(0)
    found, begun = lax.fori_loop(0, meta.shape[0] // GROUP, scan, (zero, zero))
    for u in range(GROUP):
        picked[found + u] = jnp.int32(-1)
    groups = lax.div(found + (GROUP - 1), GROUP)
    lax.fori_loop(begun, jnp.minimum(groups, RING), start, 0)
    prepare()

    def work(group, carry):
        for copy in copies(group):
            copy.wait()
        base = lax.rem(group, RING) * GROUP
        entries = [picked[group * GROUP + u] for u in range(GROUP)]
        products = [multiply(entries[u], ring.at[base + u]) for u in range(GROUP)]
        for u in range(GROUP):
            add(entries[u], products[u])

        @pl.when(group + RING < groups)
        def _():
            start(group + RING, 0)

        return carry

    lax.fori_loop(0, groups, work, 0)


def ring_scratch(slots):
    return [
        pltpu.SMEM((slots + GROUP,), jnp.int32),
        pltpu.VMEM((RING * GROUP, BLK, BLK), BF16),
        pltpu.SemaphoreType.DMA((RING * GROUP,)),
    ]


def row_at(way, i):
    count = lax.axis_size("rows")
    row = lax.axis_index("rows")
    if way == "all":
        return i
    if way == "direct":
        return lax.rem(row + (i % count), count)
    return row ^ i


def aggregate(meta, tiles, parts, owners, way, cuts, layout):
    tile_bits, source_bits, nth_bits = layout
    columns = sum(part.shape[0] for part in parts)
    sources = parts[0].shape[1] // BLK
    n_rows, per_row = lax.axis_size("rows"), cuts[-1]
    dead = n_rows * per_row
    pieces = list(zip(cuts[:-1], cuts[1:]))
    kept = (0, 2) if way == "pair" else (0,)
    shapes = [
        jax.ShapeDtypeStruct(((high - low) * BLK, columns), F32 if i in kept else BF16)
        for i in owners
        for low, high in pieces
    ]
    many = len(owners) == n_rows

    def body(meta_ref, tiles_ref, own_ref, *refs):
        part_refs = refs[: len(parts) - 1]
        outs = refs[len(parts) - 1 : len(parts) - 1 + len(shapes)]
        own, own_sem, turned, total, picked, ring, sems = refs[len(parts) - 1 + len(shapes) :]
        fetch = pltpu.make_async_copy(own_ref, own, own_sem)
        fetch.start()
        rows = [row_at(way, i) for i in owners]

        def prepare():
            fetch.wait()
            if many:
                total[...] = jnp.zeros_like(total)
            else:
                total[dead] = jnp.zeros_like(total[dead])
                for row in rows:
                    total[pl.ds(row * per_row, per_row)] = jnp.zeros((per_row, BLK, columns), F32)
            for s in range(sources):
                now = slice(s * BLK, (s + 1) * BLK)
                block = jnp.concatenate([own[:, now]] + [ref[:, now] for ref in part_refs], axis=0)
                turned[s] = jnp.transpose(block)

        def multiply(entry, tile):
            source = (jnp.maximum(entry, 0) >> tile_bits) & ((1 << source_bits) - 1)
            return jnp.dot(tile[...], turned[source], preferred_element_type=F32)

        def add(entry, product):
            rest = entry >> (tile_bits + source_bits)
            dest = (rest >> nth_bits) * per_row + (rest & ((1 << nth_bits) - 1))
            total[jnp.where(entry < 0, dead, dest)] += product

        def wanted(entry):
            if many:
                return entry >= 0
            owner = entry >> (tile_bits + source_bits + nth_bits)
            found = owner == rows[0]
            for row in rows[1:]:
                found = found | (owner == row)
            return found

        each_tile(
            meta_ref, wanted, picked, tiles_ref, ring, sems, tile_bits, prepare, multiply, add
        )
        spots = [(row * per_row + low, high - low) for row in rows for low, high in pieces]
        for out, (low, count) in zip(outs, spots):
            out[...] = total[pl.ds(low, count)].reshape(out.shape).astype(out.dtype)

    slots = tiles.shape[0]
    return call(
        body,
        "aggregate",
        shapes,
        [SMEM_SPEC, HBM_SPEC, HBM_SPEC] + [VMEM_SPEC] * (len(parts) - 1),
        [
            pltpu.VMEM(parts[0].shape, BF16),
            pltpu.SemaphoreType.DMA,
            pltpu.VMEM((sources, BLK, columns), BF16),
            pltpu.VMEM((dead + 1, BLK, columns), F32),
        ]
        + ring_scratch(tiles.shape[0]),
        slots * BLK * BLK * columns,
        slots * BLK * BLK,
    )(meta, tiles, *parts)


def spread_back(meta, tiles, pieces, columns, sources, per_row, layout, cols):
    tile_bits, source_bits, nth_bits = layout
    given = []
    for piece in pieces:
        if not any(piece[0] is other for other in given):
            given.append(piece[0])
    spare = lax.axis_size("rows") * per_row

    def body(meta_ref, tiles_ref, *refs):
        keep, send, held, total, picked, ring, sems = refs[len(given) :]

        def prepare():
            total[...] = jnp.zeros_like(total)
            held[spare] = jnp.zeros_like(held[spare])
            for array, line, way, i, first, count in pieces:
                ref = next(ref for ref, other in zip(refs, given) if other is array)
                row = row_at(way, i)
                for q in range(count):
                    held[row * per_row + first + q] = ref[
                        line : line + columns, q * BLK : (q + 1) * BLK
                    ]

        def multiply(entry, tile):
            rest = entry >> (tile_bits + source_bits)
            dest = (rest >> nth_bits) * per_row + (rest & ((1 << nth_bits) - 1))
            dest = jnp.where(entry < 0, spare, dest)
            return jnp.dot(held[dest], tile[...], preferred_element_type=F32)

        def add(entry, product):
            source = (jnp.maximum(entry, 0) >> tile_bits) & ((1 << source_bits) - 1)
            total[source] += product

        each_tile(
            meta_ref, lambda entry: entry >= 0, picked, tiles_ref, ring, sems, tile_bits,
            prepare, multiply, add,
        )
        for s in range(sources):
            keep[:, s * BLK : (s + 1) * BLK] = total[s, :cols, :]
            send[:, s * BLK : (s + 1) * BLK] = total[s, cols:, :].astype(BF16)

    slots = tiles.shape[0]
    return call(
        body,
        "spread_back",
        [
            jax.ShapeDtypeStruct((cols, sources * BLK), F32),
            jax.ShapeDtypeStruct((cols, sources * BLK), BF16),
        ],
        [SMEM_SPEC, HBM_SPEC] + [VMEM_SPEC] * len(given),
        [
            pltpu.VMEM((spare + 1, columns, BLK), BF16),
            pltpu.VMEM((sources, columns, BLK), F32),
        ]
        + ring_scratch(tiles.shape[0]),
        slots * BLK * BLK * columns,
        slots * BLK * BLK,
    )(meta, tiles, *given)


def spot_order(chips):
    at = lax.axis_index("wide")
    chip, core = at >> 1, at & 1
    return [
        2 * lax.rem(chip + s, chips) + (core if k == 0 else 1 - core) for s in range(chips) for k in range(2)
    ]


def layer(near, far, weight, bias, cotangent, cols, chips):
    rows, hidden = cotangent.shape
    near_cols = near[0].shape[1]
    step = 2 * BLK if rows % (2 * BLK) == 0 else BLK

    def body(*refs):
        near_refs = refs[: len(near)]
        far_refs = refs[len(near) : len(near) + len(far)]
        weight_ref, bias_ref, cot_ref = refs[len(near) + len(far) : len(near) + len(far) + 3]
        act_ref, near_out, far_out, near_mix, far_mix, delta_ref, ordered = refs[
            len(near) + len(far) + 3 :
        ]
        for part, owner in enumerate(spot_order(chips)):
            low = pl.multiple_of(owner * cols, cols)
            ordered[part * cols : (part + 1) * cols, :] = weight_ref[pl.ds(low, cols), :]
        for low in range(0, rows, step):
            now = slice(low, low + step)
            mixed = []
            for group, out in ((near_refs, near_mix), (far_refs, far_mix)):
                value = group[0][now, :].astype(F32)
                for ref in group[1:]:
                    value = value + ref[now, :].astype(F32)
                mixed.append(value.astype(BF16))
                out[now, :] = mixed[-1]
            pre = jnp.dot(mixed[0], ordered[:near_cols, :], preferred_element_type=F32)
            pre = pre + jnp.dot(mixed[1], ordered[near_cols:, :], preferred_element_type=F32)
            pre = pre + bias_ref[...].astype(F32)
            square = pre * pre
            bend = jnp.tanh(ROOT * pre * (1.0 + CUBIC * square))
            half = 0.5 * (1.0 + bend)
            act_ref[now, :] = (pre * half).astype(BF16)
            slope = half + 0.5 * ROOT * pre * (1.0 - bend * bend) * (1.0 + 3.0 * CUBIC * square)
            delta = (cot_ref[now, :].astype(F32) * slope).astype(BF16)
            delta_ref[now, :] = delta
            turned = lax.dot_general(
                ordered[...], delta, (((1,), (1,)), ((), ())), preferred_element_type=F32
            ).astype(BF16)
            near_out[:, now] = turned[:near_cols, :]
            far_out[:, now] = turned[near_cols:, :]

    return call(
        body,
        "layer",
        [
            jax.ShapeDtypeStruct((rows, hidden), BF16),
            jax.ShapeDtypeStruct((near_cols, rows), BF16),
            jax.ShapeDtypeStruct((hidden - near_cols, rows), BF16),
            jax.ShapeDtypeStruct((rows, near_cols), BF16),
            jax.ShapeDtypeStruct((rows, hidden - near_cols), BF16),
            jax.ShapeDtypeStruct((rows, hidden), BF16),
        ],
        [VMEM_SPEC] * (len(near) + len(far) + 3),
        [pltpu.VMEM((hidden, hidden), BF16)],
        4 * rows * hidden * hidden,
        10 * rows * hidden,
    )(*near, *far, weight, bias, cotangent)


def weight_parts(near_mix, far_mix, delta, cols, chips):
    rows, near_cols = near_mix.shape
    hidden = delta.shape[1]
    lines = cols + 8

    def body(near_ref, far_ref, delta_ref, grad_ref):
        tail = jnp.broadcast_to(
            jnp.sum(delta_ref[...].astype(F32), axis=0, keepdims=True), (8, hidden)
        )
        grads = [
            lax.dot_general(
                ref[...], delta_ref[...], (((0,), (0,)), ((), ())), preferred_element_type=F32
            )
            for ref in (near_ref, far_ref)
        ]
        for part in range(2 * chips):
            source = grads[0] if part < 2 else grads[1]
            low = part * cols - (0 if part < 2 else near_cols)
            grad_ref[part % 2, part // 2, :cols, :] = source[low : low + cols, :]
            grad_ref[part % 2, part // 2, cols:, :] = tail

    return call(
        body,
        "weight_parts",
        [jax.ShapeDtypeStruct((2, chips, lines, hidden), F32)],
        [VMEM_SPEC] * 3,
        [],
        2 * rows * hidden * hidden,
        6 * rows * hidden,
    )(near_mix, far_mix, delta)[0]


def weight_sums(gathered, n_rows, top, lines, packed, hidden):
    tall, width = gathered.shape[0] // n_rows, gathered.shape[1] // hidden

    def body(ref, out):
        for k in range(width):
            rows = min(packed, lines - k * packed)
            if rows > 0:
                value = jnp.zeros((packed, hidden), F32)
                for row in range(n_rows):
                    low = row * tall + top
                    part = ref[low : low + packed, k * hidden : (k + 1) * hidden]
                    value = value + part.astype(F32)
                out[k * packed : k * packed + rows, :] = value[:rows]

    return call(
        body,
        "weight_sums",
        [jax.ShapeDtypeStruct((lines, hidden), F32)],
        [VMEM_SPEC],
        [],
        0,
        8 * lines * hidden,
    )(gathered)[0]


def assemble(keep, got, mine, other, cols, chips):
    hidden = mine[0].shape[1]

    def body(keep_ref, got_ref, *refs):
        grad_ref, out, bias_out = refs[-3:]
        grad_ref[...] = (keep_ref[...] + got_ref[...].astype(F32)).astype(BF16)
        for part, owner in enumerate(spot_order(chips)):
            low = pl.multiple_of(owner * cols, cols)
            out[pl.ds(low, cols), :] = refs[(part % 2) * chips + part // 2][:cols, :]
        bias_out[...] = refs[0][cols : cols + 1, :]

    return call(
        body,
        "assemble",
        [
            jax.ShapeDtypeStruct(keep.shape, BF16),
            jax.ShapeDtypeStruct((2 * chips * cols, hidden), F32),
            jax.ShapeDtypeStruct((1, hidden), F32),
        ],
        [VMEM_SPEC] * (2 + 2 * chips),
        [],
        0,
        8 * chips * cols * hidden,
    )(keep, got, *mine, *other)


def per_device(features, tile_weights, tile_source, tile_dest, tile_count, weight, bias, cotangent):
    cols, width = features.shape
    sources = width // BLK
    slots = tile_weights.shape[0]
    hidden = weight.shape[0]
    wide = lax.axis_size("wide")
    chips = wide // 2
    n_rows = lax.axis_size("rows")
    paired = n_rows == 4
    chunk = sources // wide
    per_row = chips * chunk
    near_cols = 2 * cols
    lines = cols + 8

    at = lax.axis_index("wide")
    chip, core = at >> 1, at & 1

    def swap_cores(value):
        return lax.ppermute(value, "wide", [(i, i ^ 1) for i in range(wide)])

    def from_chip(value, shift):
        pairs = [(2 * ((i + shift) % chips) + k, 2 * i + k) for i in range(chips) for k in range(2)]
        return lax.ppermute(value, "wide", pairs)

    def around(value, shift):
        return lax.ppermute(value, "rows", [(i, (i + shift) % n_rows) for i in range(n_rows)])

    def beside(value):
        return lax.ppermute(value, "rows", [(i, i ^ 1) for i in range(n_rows)])

    def across(value):
        return lax.ppermute(value, "rows", [(i, i ^ 2) for i in range(n_rows)])

    def tied(value, other):
        return lax.optimization_barrier((value, other))[0]

    parts = [features, swap_cores(features)]
    layout = tile_bits, source_bits, nth_bits = bits_of(slots), bits_of(sources), bits_of(per_row)

    def split(value, size):
        whole = ((value.astype(F32) + 0.5) * (1.0 / size)).astype(jnp.int32)
        return whole, value - whole * size

    slot = jnp.arange(slots, dtype=jnp.int32)
    owner, within = split(tile_dest, sources)
    holder, nth = split(within, chunk)
    away = (holder >> 1) - chip
    away = jnp.where(away < 0, away + chips, away)
    place = (owner << nth_bits) | (away * chunk + nth)
    ours = (slot < tile_count[0]) & ((holder & 1) == core)
    meta = (place << (source_bits + tile_bits)) | (tile_source << tile_bits) | slot
    meta = jnp.where(ours, meta, -1)

    def partial_sums(owners, way, cuts):
        return aggregate(meta, tile_weights, parts, owners, way, cuts, layout)

    cuts = (0, chunk, per_row)
    if paired:

        def merged(value, other):
            return (value.astype(F32) + other.astype(F32)).astype(BF16)

        (relayed,) = partial_sums([3], "pair", (0, per_row))
        near_1, far_1, near_2, far_2 = partial_sums([1, 2], "pair", cuts)
        near_0, far_0 = partial_sums([0], "pair", cuts)
        passed = beside(relayed)
        edge = chunk * BLK
        far_terms = [far_0, beside(far_1), across(merged(far_2, passed[edge:]))]
        near = [near_0, beside(near_1), across(merged(near_2, passed[:edge]))]
    else:
        outs = partial_sums(list(range(n_rows)), "direct", cuts)
        near = [outs[0]] + [around(outs[2 * s], s) for s in range(1, n_rows)]
        far_terms = [outs[1]] + [around(outs[2 * s + 1], s) for s in range(1, n_rows)]
    passing = far_terms[0]
    for term in far_terms[1:]:
        passing = passing + term.astype(F32)
    passing = passing.astype(BF16).reshape(chips - 1, chunk * BLK, near_cols)
    far = [from_chip(passing[chips - s - 1], s) for s in range(1, chips)]
    far = far[0] if chips == 2 else jnp.concatenate(far, axis=1)

    activation, near_prop, far_prop, near_mix, far_mix, delta = layer(
        near, [far], weight, bias.reshape(1, hidden), cotangent, cols, chips
    )

    far_prop = far_prop.reshape(chips - 1, near_cols, chunk * BLK)
    coming = [from_chip(far_prop[chips - s - 1], s) for s in range(1, chips)]
    coming = coming[0] if chips == 2 else jnp.concatenate(coming, axis=1)
    if paired:
        got_skip = across(near_prop)
        got_next = beside(near_prop)
        got_last = beside(tied(got_skip, coming))
        near_all = [near_prop, got_next, got_skip, got_last]
    else:
        near_all = [near_prop] + [around(near_prop, -s) for s in range(1, n_rows)]

    grads = weight_parts(near_mix, far_mix, delta, cols, chips)
    part = grads[0] + swap_cores(grads[1])
    quarter = part[0]
    for s in range(1, chips):
        quarter = quarter + from_chip(part[chips - s], s)
    width_in = coming.shape[1] // hidden
    packed = -(-lines // width_in)
    extra = jnp.pad(quarter.astype(BF16), ((0, width_in * packed - lines), (0, 0)))
    extra = jnp.concatenate([extra[k * packed : (k + 1) * packed] for k in range(width_in)], axis=1)
    extra = jnp.pad(extra, ((0, -packed % 8), (0, 0)))
    tall = near_cols + extra.shape[0]
    far_all = lax.all_gather(jnp.concatenate([coming, extra], axis=0), "rows", axis=0, tiled=True)

    way = "pair" if paired else "direct"
    pieces = [(array, 0, way, i, 0, chunk) for i, array in enumerate(near_all)]
    pieces += [(far_all, i * tall, "all", i, chunk, per_row - chunk) for i in range(n_rows)]
    keep, send = spread_back(
        meta, tile_weights, pieces, near_cols, sources, per_row, layout, cols
    )
    got = swap_cores(send)
    quarter = weight_sums(far_all, n_rows, near_cols, lines, packed, hidden)
    half = [quarter] + [from_chip(quarter, s) for s in range(1, chips)]
    other = swap_cores(jnp.stack(half))
    grad_features, grad_weight, grad_bias = assemble(
        keep, got, half, [other[s] for s in range(chips)], cols, chips
    )
    return (activation, grad_features, grad_weight, grad_bias.reshape(hidden))


def solution(mesh):
    in_specs = (
        P("wide", ("groups", "rows")),
        P(("groups", "rows"), None, None),
        P(("groups", "rows")),
        P(("groups", "rows")),
        P(("groups", "rows")),
        P(),
        P(),
        P(("groups", "rows", "wide"), None),
    )
    out_specs = (
        P(("groups", "rows", "wide"), None),
        P("wide", ("groups", "rows")),
        P("groups", None),
        P("groups"),
    )
    return jax.shard_map(
        per_device, mesh=mesh, in_specs=in_specs, out_specs=out_specs, check_vma=False
    )
```

```python
import math

import jax
import jax.numpy as jnp
from jax import lax
from jax.experimental import pallas as pl
from jax.experimental.pallas import tpu as pltpu
from jax.sharding import PartitionSpec as P

BLK = 128
GROUP = 16
RING = 4
VMEM_BYTES = 48 * 1024 * 1024
ROOT = math.sqrt(2.0 / math.pi)
CUBIC = 0.044715
BF16 = jnp.bfloat16
F32 = jnp.float32

SMEM_SPEC = pl.BlockSpec(memory_space=pltpu.SMEM)
VMEM_SPEC = pl.BlockSpec(memory_space=pltpu.VMEM)
HBM_SPEC = pl.BlockSpec(memory_space=pltpu.HBM)


def bits_of(size):
    return max(1, int(size).bit_length())


def call(body, name, out_shape, in_specs, scratch, flops, nbytes):
    return pl.pallas_call(
        body,
        name=name,
        out_shape=out_shape,
        in_specs=in_specs,
        out_specs=jax.tree.map(lambda _: VMEM_SPEC, out_shape),
        scratch_shapes=scratch,
        compiler_params=pltpu.CompilerParams(vmem_limit_bytes=VMEM_BYTES),
        cost_estimate=pl.CostEstimate(flops=flops, bytes_accessed=nbytes, transcendentals=0),
    )


def each_tile(meta, wanted, picked, tiles, ring, sems, tile_bits, prepare, multiply, add):
    tile_mask = (1 << tile_bits) - 1

    def copies(group):
        base = lax.rem(group, RING) * GROUP
        for u in range(GROUP):
            tile = jnp.maximum(picked[group * GROUP + u], 0) & tile_mask
            yield pltpu.make_async_copy(tiles.at[tile], ring.at[base + u], sems.at[base + u])

    def start(group, carry):
        for copy in copies(group):
            copy.start()
        return carry

    def scan(step, state):
        found, begun = state
        for u in range(GROUP):
            entry = meta[step * GROUP + u]
            picked[found] = entry
            found = found + jnp.where(wanted(entry), 1, 0)
        full = (found >= (begun + 1) * GROUP) & (begun < RING)

        @pl.when(full)
        def _():
            start(begun, 0)

        return found, begun + jnp.where(full, 1, 0)

    zero = jnp.int32(0)
    found, begun = lax.fori_loop(0, meta.shape[0] // GROUP, scan, (zero, zero))
    for u in range(GROUP):
        picked[found + u] = jnp.int32(-1)
    groups = lax.div(found + (GROUP - 1), GROUP)
    lax.fori_loop(begun, jnp.minimum(groups, RING), start, 0)
    prepare()

    def work(group, carry):
        for copy in copies(group):
            copy.wait()
        base = lax.rem(group, RING) * GROUP
        entries = [picked[group * GROUP + u] for u in range(GROUP)]
        products = [multiply(entries[u], ring.at[base + u]) for u in range(GROUP)]
        for u in range(GROUP):
            add(entries[u], products[u])

        @pl.when(group + RING < groups)
        def _():
            start(group + RING, 0)

        return carry

    lax.fori_loop(0, groups, work, 0)


def ring_scratch(slots):
    return [
        pltpu.SMEM((slots + GROUP,), jnp.int32),
        pltpu.VMEM((RING * GROUP, BLK, BLK), BF16),
        pltpu.SemaphoreType.DMA((RING * GROUP,)),
    ]


def row_at(way, i):
    count = lax.axis_size("rows")
    row = lax.axis_index("rows")
    if way == "all":
        return i
    if way == "direct":
        return lax.rem(row + (i % count), count)
    return row ^ i


def aggregate(meta, tiles, parts, owners, way, cuts, layout):
    tile_bits, source_bits, nth_bits = layout
    columns = sum(part.shape[0] for part in parts)
    sources = parts[0].shape[1] // BLK
    n_rows, per_row = lax.axis_size("rows"), cuts[-1]
    dead = n_rows * per_row
    pieces = list(zip(cuts[:-1], cuts[1:]))
    kept = (0, 2) if way == "pair" else (0,)
    shapes = [
        jax.ShapeDtypeStruct(((high - low) * BLK, columns), F32 if i in kept else BF16)
        for i in owners
        for low, high in pieces
    ]
    many = len(owners) == n_rows

    def body(meta_ref, tiles_ref, *refs):
        part_refs = refs[: len(parts)]
        outs = refs[len(parts) : len(parts) + len(shapes)]
        turned, total, picked, ring, sems = refs[len(parts) + len(shapes) :]
        rows = [row_at(way, i) for i in owners]

        def prepare():
            if many:
                total[...] = jnp.zeros_like(total)
            else:
                total[dead] = jnp.zeros_like(total[dead])
                for row in rows:
                    total[pl.ds(row * per_row, per_row)] = jnp.zeros((per_row, BLK, columns), F32)
            for s in range(sources):
                now = slice(s * BLK, (s + 1) * BLK)
                block = jnp.concatenate([ref[:, now] for ref in part_refs], axis=0)
                turned[s] = jnp.transpose(block)

        def multiply(entry, tile):
            source = (jnp.maximum(entry, 0) >> tile_bits) & ((1 << source_bits) - 1)
            return jnp.dot(tile[...], turned[source], preferred_element_type=F32)

        def add(entry, product):
            rest = entry >> (tile_bits + source_bits)
            dest = (rest >> nth_bits) * per_row + (rest & ((1 << nth_bits) - 1))
            total[jnp.where(entry < 0, dead, dest)] += product

        def wanted(entry):
            if many:
                return entry >= 0
            owner = entry >> (tile_bits + source_bits + nth_bits)
            found = owner == rows[0]
            for row in rows[1:]:
                found = found | (owner == row)
            return found

        each_tile(
            meta_ref, wanted, picked, tiles_ref, ring, sems, tile_bits, prepare, multiply, add
        )
        spots = [(row * per_row + low, high - low) for row in rows for low, high in pieces]
        for out, (low, count) in zip(outs, spots):
            out[...] = total[pl.ds(low, count)].reshape(out.shape).astype(out.dtype)

    slots = tiles.shape[0]
    return call(
        body,
        "aggregate",
        shapes,
        [SMEM_SPEC, HBM_SPEC] + [VMEM_SPEC] * len(parts),
        [
            pltpu.VMEM((sources, BLK, columns), BF16),
            pltpu.VMEM((dead + 1, BLK, columns), F32),
        ]
        + ring_scratch(tiles.shape[0]),
        slots * BLK * BLK * columns,
        slots * BLK * BLK,
    )(meta, tiles, *parts)


def spread_back(meta, tiles, pieces, columns, sources, per_row, layout, cols):
    tile_bits, source_bits, nth_bits = layout
    given = []
    for piece in pieces:
        if not any(piece[0] is other for other in given):
            given.append(piece[0])
    spare = lax.axis_size("rows") * per_row

    def body(meta_ref, tiles_ref, *refs):
        keep, send, held, total, picked, ring, sems = refs[len(given) :]

        def prepare():
            total[...] = jnp.zeros_like(total)
            held[spare] = jnp.zeros_like(held[spare])
            for array, line, way, i, first, count in pieces:
                ref = next(ref for ref, other in zip(refs, given) if other is array)
                row = row_at(way, i)
                for q in range(count):
                    held[row * per_row + first + q] = ref[
                        line : line + columns, q * BLK : (q + 1) * BLK
                    ]

        def multiply(entry, tile):
            rest = entry >> (tile_bits + source_bits)
            dest = (rest >> nth_bits) * per_row + (rest & ((1 << nth_bits) - 1))
            dest = jnp.where(entry < 0, spare, dest)
            return jnp.dot(held[dest], tile[...], preferred_element_type=F32)

        def add(entry, product):
            source = (jnp.maximum(entry, 0) >> tile_bits) & ((1 << source_bits) - 1)
            total[source] += product

        each_tile(
            meta_ref, lambda entry: entry >= 0, picked, tiles_ref, ring, sems, tile_bits,
            prepare, multiply, add,
        )
        for s in range(sources):
            keep[:, s * BLK : (s + 1) * BLK] = total[s, :cols, :]
            send[:, s * BLK : (s + 1) * BLK] = total[s, cols:, :].astype(BF16)

    slots = tiles.shape[0]
    return call(
        body,
        "spread_back",
        [
            jax.ShapeDtypeStruct((cols, sources * BLK), F32),
            jax.ShapeDtypeStruct((cols, sources * BLK), BF16),
        ],
        [SMEM_SPEC, HBM_SPEC] + [VMEM_SPEC] * len(given),
        [
            pltpu.VMEM((spare + 1, columns, BLK), BF16),
            pltpu.VMEM((sources, columns, BLK), F32),
        ]
        + ring_scratch(tiles.shape[0]),
        slots * BLK * BLK * columns,
        slots * BLK * BLK,
    )(meta, tiles, *given)


def spot_order(chips):
    at = lax.axis_index("wide")
    chip, core = at >> 1, at & 1
    return [
        2 * lax.rem(chip + s, chips) + (core if k == 0 else 1 - core) for s in range(chips) for k in range(2)
    ]


def layer(near, far, weight, bias, cotangent, cols, chips):
    rows, hidden = cotangent.shape
    near_cols = near[0].shape[1]
    step = 2 * BLK if rows % (2 * BLK) == 0 else BLK

    def body(*refs):
        near_refs = refs[: len(near)]
        far_refs = refs[len(near) : len(near) + len(far)]
        weight_ref, bias_ref, cot_ref = refs[len(near) + len(far) : len(near) + len(far) + 3]
        act_ref, near_out, far_out, near_mix, far_mix, delta_ref, ordered = refs[
            len(near) + len(far) + 3 :
        ]
        for part, owner in enumerate(spot_order(chips)):
            low = pl.multiple_of(owner * cols, cols)
            ordered[part * cols : (part + 1) * cols, :] = weight_ref[pl.ds(low, cols), :]
        for low in range(0, rows, step):
            now = slice(low, low + step)
            mixed = []
            for group, out in ((near_refs, near_mix), (far_refs, far_mix)):
                value = group[0][now, :].astype(F32)
                for ref in group[1:]:
                    value = value + ref[now, :].astype(F32)
                mixed.append(value.astype(BF16))
                out[now, :] = mixed[-1]
            pre = jnp.dot(mixed[0], ordered[:near_cols, :], preferred_element_type=F32)
            pre = pre + jnp.dot(mixed[1], ordered[near_cols:, :], preferred_element_type=F32)
            pre = pre + bias_ref[...].astype(F32)
            square = pre * pre
            bend = jnp.tanh(ROOT * pre * (1.0 + CUBIC * square))
            half = 0.5 * (1.0 + bend)
            act_ref[now, :] = (pre * half).astype(BF16)
            slope = half + 0.5 * ROOT * pre * (1.0 - bend * bend) * (1.0 + 3.0 * CUBIC * square)
            delta = (cot_ref[now, :].astype(F32) * slope).astype(BF16)
            delta_ref[now, :] = delta
            turned = lax.dot_general(
                ordered[...], delta, (((1,), (1,)), ((), ())), preferred_element_type=F32
            ).astype(BF16)
            near_out[:, now] = turned[:near_cols, :]
            far_out[:, now] = turned[near_cols:, :]

    return call(
        body,
        "layer",
        [
            jax.ShapeDtypeStruct((rows, hidden), BF16),
            jax.ShapeDtypeStruct((near_cols, rows), BF16),
            jax.ShapeDtypeStruct((hidden - near_cols, rows), BF16),
            jax.ShapeDtypeStruct((rows, near_cols), BF16),
            jax.ShapeDtypeStruct((rows, hidden - near_cols), BF16),
            jax.ShapeDtypeStruct((rows, hidden), BF16),
        ],
        [VMEM_SPEC] * (len(near) + len(far) + 3),
        [pltpu.VMEM((hidden, hidden), BF16)],
        4 * rows * hidden * hidden,
        10 * rows * hidden,
    )(*near, *far, weight, bias, cotangent)


def weight_parts(near_mix, far_mix, delta, cols, chips):
    rows, near_cols = near_mix.shape
    hidden = delta.shape[1]
    lines = cols + 8

    def body(near_ref, far_ref, delta_ref, grad_ref):
        tail = jnp.broadcast_to(
            jnp.sum(delta_ref[...].astype(F32), axis=0, keepdims=True), (8, hidden)
        )
        grads = [
            lax.dot_general(
                ref[...], delta_ref[...], (((0,), (0,)), ((), ())), preferred_element_type=F32
            )
            for ref in (near_ref, far_ref)
        ]
        for part in range(2 * chips):
            source = grads[0] if part < 2 else grads[1]
            low = part * cols - (0 if part < 2 else near_cols)
            grad_ref[part % 2, part // 2, :cols, :] = source[low : low + cols, :]
            grad_ref[part % 2, part // 2, cols:, :] = tail

    return call(
        body,
        "weight_parts",
        [jax.ShapeDtypeStruct((2, chips, lines, hidden), F32)],
        [VMEM_SPEC] * 3,
        [],
        2 * rows * hidden * hidden,
        6 * rows * hidden,
    )(near_mix, far_mix, delta)[0]


def weight_sums(gathered, n_rows, top, lines, packed, hidden):
    tall, width = gathered.shape[0] // n_rows, gathered.shape[1] // hidden

    def body(ref, out):
        for k in range(width):
            rows = min(packed, lines - k * packed)
            if rows > 0:
                value = jnp.zeros((packed, hidden), F32)
                for row in range(n_rows):
                    low = row * tall + top
                    part = ref[low : low + packed, k * hidden : (k + 1) * hidden]
                    value = value + part.astype(F32)
                out[k * packed : k * packed + rows, :] = value[:rows]

    return call(
        body,
        "weight_sums",
        [jax.ShapeDtypeStruct((lines, hidden), F32)],
        [VMEM_SPEC],
        [],
        0,
        8 * lines * hidden,
    )(gathered)[0]


def assemble(keep, got, mine, other, cols, chips):
    hidden = mine[0].shape[1]

    def body(keep_ref, got_ref, *refs):
        grad_ref, out, bias_out = refs[-3:]
        grad_ref[...] = (keep_ref[...] + got_ref[...].astype(F32)).astype(BF16)
        for part, owner in enumerate(spot_order(chips)):
            low = pl.multiple_of(owner * cols, cols)
            out[pl.ds(low, cols), :] = refs[(part % 2) * chips + part // 2][:cols, :]
        bias_out[...] = refs[0][cols : cols + 1, :]

    return call(
        body,
        "assemble",
        [
            jax.ShapeDtypeStruct(keep.shape, BF16),
            jax.ShapeDtypeStruct((2 * chips * cols, hidden), F32),
            jax.ShapeDtypeStruct((1, hidden), F32),
        ],
        [VMEM_SPEC] * (2 + 2 * chips),
        [],
        0,
        8 * chips * cols * hidden,
    )(keep, got, *mine, *other)


def per_device(features, tile_weights, tile_source, tile_dest, tile_count, weight, bias, cotangent):
    cols, width = features.shape
    sources = width // BLK
    slots = tile_weights.shape[0]
    hidden = weight.shape[0]
    wide = lax.axis_size("wide")
    chips = wide // 2
    n_rows = lax.axis_size("rows")
    paired = n_rows == 4
    chunk = sources // wide
    per_row = chips * chunk
    near_cols = 2 * cols
    lines = cols + 8

    at = lax.axis_index("wide")
    chip, core = at >> 1, at & 1

    def swap_cores(value):
        return lax.ppermute(value, "wide", [(i, i ^ 1) for i in range(wide)])

    def from_chip(value, shift):
        pairs = [(2 * ((i + shift) % chips) + k, 2 * i + k) for i in range(chips) for k in range(2)]
        return lax.ppermute(value, "wide", pairs)

    def around(value, shift):
        return lax.ppermute(value, "rows", [(i, (i + shift) % n_rows) for i in range(n_rows)])

    def beside(value):
        return lax.ppermute(value, "rows", [(i, i ^ 1) for i in range(n_rows)])

    def across(value):
        return lax.ppermute(value, "rows", [(i, i ^ 2) for i in range(n_rows)])

    def tied(value, other):
        return lax.optimization_barrier((value, other))[0]

    parts = [features, swap_cores(features)]
    layout = tile_bits, source_bits, nth_bits = bits_of(slots), bits_of(sources), bits_of(per_row)

    def split(value, size):
        whole = ((value.astype(F32) + 0.5) * (1.0 / size)).astype(jnp.int32)
        return whole, value - whole * size

    slot = jnp.arange(slots, dtype=jnp.int32)
    owner, within = split(tile_dest, sources)
    holder, nth = split(within, chunk)
    away = (holder >> 1) - chip
    away = jnp.where(away < 0, away + chips, away)
    place = (owner << nth_bits) | (away * chunk + nth)
    ours = (slot < tile_count[0]) & ((holder & 1) == core)
    meta = (place << (source_bits + tile_bits)) | (tile_source << tile_bits) | slot
    meta = jnp.where(ours, meta, -1)

    def partial_sums(owners, way, cuts):
        return aggregate(meta, tile_weights, parts, owners, way, cuts, layout)

    cuts = (0, chunk, per_row)
    if paired:

        def merged(value, other):
            return (value.astype(F32) + other.astype(F32)).astype(BF16)

        (relayed,) = partial_sums([3], "pair", (0, per_row))
        near_1, far_1, near_2, far_2 = partial_sums([1, 2], "pair", cuts)
        near_0, far_0 = partial_sums([0], "pair", cuts)
        passed = beside(relayed)
        edge = chunk * BLK
        far_terms = [far_0, beside(far_1), across(merged(far_2, passed[edge:]))]
        near = [near_0, beside(near_1), across(merged(near_2, passed[:edge]))]
    else:
        outs = partial_sums(list(range(n_rows)), "direct", cuts)
        near = [outs[0]] + [around(outs[2 * s], s) for s in range(1, n_rows)]
        far_terms = [outs[1]] + [around(outs[2 * s + 1], s) for s in range(1, n_rows)]
    passing = far_terms[0]
    for term in far_terms[1:]:
        passing = passing + term.astype(F32)
    passing = passing.astype(BF16).reshape(chips - 1, chunk * BLK, near_cols)
    far = [from_chip(passing[chips - s - 1], s) for s in range(1, chips)]
    far = far[0] if chips == 2 else jnp.concatenate(far, axis=1)

    activation, near_prop, far_prop, near_mix, far_mix, delta = layer(
        near, [far], weight, bias.reshape(1, hidden), cotangent, cols, chips
    )

    far_prop = far_prop.reshape(chips - 1, near_cols, chunk * BLK)
    coming = [from_chip(far_prop[chips - s - 1], s) for s in range(1, chips)]
    coming = coming[0] if chips == 2 else jnp.concatenate(coming, axis=1)
    if paired:
        got_skip = across(near_prop)
        got_next = beside(near_prop)
        got_last = beside(tied(got_skip, coming))
        near_all = [near_prop, got_next, got_skip, got_last]
    else:
        near_all = [near_prop] + [around(near_prop, -s) for s in range(1, n_rows)]

    grads = weight_parts(near_mix, far_mix, delta, cols, chips)
    part = grads[0] + swap_cores(grads[1])
    quarter = part[0]
    for s in range(1, chips):
        quarter = quarter + from_chip(part[chips - s], s)
    width_in = coming.shape[1] // hidden
    packed = -(-lines // width_in)
    extra = jnp.pad(quarter.astype(BF16), ((0, width_in * packed - lines), (0, 0)))
    extra = jnp.concatenate([extra[k * packed : (k + 1) * packed] for k in range(width_in)], axis=1)
    extra = jnp.pad(extra, ((0, -packed % 8), (0, 0)))
    tall = near_cols + extra.shape[0]
    far_all = lax.all_gather(jnp.concatenate([coming, extra], axis=0), "rows", axis=0, tiled=True)

    way = "pair" if paired else "direct"
    pieces = [(array, 0, way, i, 0, chunk) for i, array in enumerate(near_all)]
    pieces += [(far_all, i * tall, "all", i, chunk, per_row - chunk) for i in range(n_rows)]
    keep, send = spread_back(
        meta, tile_weights, pieces, near_cols, sources, per_row, layout, cols
    )
    got = swap_cores(send)
    quarter = weight_sums(far_all, n_rows, near_cols, lines, packed, hidden)
    half = [quarter] + [from_chip(quarter, s) for s in range(1, chips)]
    other = swap_cores(jnp.stack(half))
    grad_features, grad_weight, grad_bias = assemble(
        keep, got, half, [other[s] for s in range(chips)], cols, chips
    )
    return (activation, grad_features, grad_weight, grad_bias.reshape(hidden))


def solution(mesh):
    in_specs = (
        P("wide", ("groups", "rows")),
        P(("groups", "rows"), None, None),
        P(("groups", "rows")),
        P(("groups", "rows")),
        P(("groups", "rows")),
        P(),
        P(),
        P(("groups", "rows", "wide"), None),
    )
    out_specs = (
        P(("groups", "rows", "wide"), None),
        P("wide", ("groups", "rows")),
        P("groups", None),
        P("groups"),
    )
    return jax.shard_map(
        per_device, mesh=mesh, in_specs=in_specs, out_specs=out_specs, check_vma=False
    )
```
